128 devices in a mesh: gx: 16 (over x, z), gy: 8 (over y, core).
Axes of the slice: x: 4, y: 4, z: 4, core: 2. Of those that a mesh axis runs over, the one named last changes fastest.
Arguments:
- right_side: float32 [64, 64, 512], P('gx', 'gy'), may hold values from -8 to 8
- permeability: float32 [64, 64, 512], P('gx', 'gy'), may hold values from 0.001 to 1000
- accumulation: float32 [64, 64, 512], P('gx', 'gy'), may hold values from 0.001 to 0.1
- active: int32 [64, 64, 512], P('gx', 'gy'), may hold values 0 or 1
- fault_local: int32 [128, 128, 128], P(('gx', 'gy')), may hold values from 0 to 16383
- fault_remote: int32 [128, 128, 128], P(('gx', 'gy')), may hold values from 0 to 16383
- fault_count: int32 [128, 128], P(('gx', 'gy')), may hold values from 0 to 128, as said below
- fault_mult: float32 [128, 128, 128], P(('gx', 'gy')), may hold values from 0.3 to 1
- low_bound: float32 [1], replicated, may hold values from 0.02 to 0.1
- high_bound: float32 [1], replicated, may hold values from 1.8 to 2
Outputs:
- correction: float32 [64, 64, 512], P('gx', 'gy')
- residual: float32 [64, 64, 512], P('gx', 'gy')
The draws below stay inside these ranges and needn't reach their ends.
Inputs may be any that keep to these rules, and one draw needn't show every extreme that they name: `fault_local`: a cell of the owner's block, numbered with layers fastest; slots at or beyond the block's count carry no connection. `fault_remote`: a cell of the remote owner's block, numbered likewise. `fault_count`: some block is full.
All inputs are finite; a program needn't handle non-finite values. No bound on the sum of `active` on one device may be relied on, other than what follows from the above.
Results may differ from the reference program's by a relative error of at most 0.000021.
Values sent between devices are 32-bit elements; how exact they have to be, the bound alone decides.
A program may use at most 64 MiB of HBM per device.

```python
import math
import jax
import jax.numpy as jnp

CX = 4
CY = 8
NZ = 512
FACES = 128
ITERS = 3
OWNERS = 128
NX = 64
NY = 64
N_GY = 8


def draw_fault_count(key, part):
    key = jax.random.fold_in(key, 7)
    key_heavy, key_base, key_spot = jax.random.split(key, 3)
    heavy = jnp.left_shift(jnp.int32(1), jax.random.randint(key_heavy, (OWNERS, 1), 0, 4))
    base = jax.random.randint(key_base, (OWNERS, OWNERS), 0, FACES // 2 + 1)
    counts = jnp.minimum(base * heavy, FACES).reshape(-1)
    spot = jax.random.randint(key_spot, (), 0, OWNERS * OWNERS)
    places = jnp.arange(OWNERS * OWNERS, dtype=jnp.int32)
    counts = jnp.where(places == spot, FACES, counts)
    return counts.reshape(OWNERS, OWNERS).astype(jnp.int32)


def set_ends(drawn, rng, low, high):
    longest = drawn.shape.index(max(drawn.shape))
    spots = []
    for shift in (0, 1):
        where = [jax.random.randint(jax.random.fold_in(rng, axis), (), 0, length) for axis, length in enumerate(drawn.shape)]
        where[longest] = (where[longest] + shift) % drawn.shape[longest]
        spots.append(tuple(where))
    return drawn.at[spots[0]].set(low).at[spots[1]].set(high)


def block_levels(own_key, extent, shards, smallest, high):
    factor_of, own = 1.0, jax.random.fold_in(own_key, 6)
    for position, shards_of in shards:
        heights = jnp.exp(jax.random.uniform(jax.random.fold_in(own, position), (shards_of,), jnp.float32, smallest / len(shards), high / len(shards)))
        factor_of = factor_of * jnp.repeat(heights, extent[position] // shards_of).reshape([-1 if axis == position else 1 for axis in range(len(extent))])
    return factor_of


def bell_draw(key, extent, width, limit, pieces=(), held_as=jnp.bfloat16):
    level = block_levels(key, extent, pieces, -0.22, 0.18) if pieces else 1.0
    array = jax.random.normal(key, extent, jnp.float32) * width * level
    return jnp.minimum(jnp.maximum(array, -limit), limit).astype(held_as)


def setup_inputs(seed: int = 0) -> dict:
    splits = jax.random.split(jax.random.key(seed), 11)
    right_side = bell_draw(splits[0], (NX, NY, NZ), 1.0, 8.0, ((0, 16), (1, 8)), jnp.float32)
    permeability = jnp.clip(jnp.exp(math.log(1000.0) - 13.815511 * jax.random.uniform(splits[1], (NX, NY, NZ), jnp.float32) ** block_levels(splits[1], (NX, NY, NZ), ((0, 16), (1, 8)), -0.2, 0.2)), 0.001, 1000.0)
    accumulation = jnp.clip(jnp.exp(math.log(0.1) - 4.6051702 * jax.random.uniform(splits[2], (NX, NY, NZ), jnp.float32) ** block_levels(splits[2], (NX, NY, NZ), ((0, 16), (1, 8)), -0.2, 0.2)), 0.001, 0.1)
    active = set_ends((jax.random.randint(splits[3], (NX, NY, NZ), 0, 10) < 9).astype(jnp.int32), jax.random.fold_in(splits[3], 1), 0, 1)
    fault_local = set_ends(jax.random.randint(splits[4], (OWNERS, OWNERS, FACES), 0, CX * CY * NZ), jax.random.fold_in(splits[4], 1), 0, (CX * CY * NZ) - 1).astype(jnp.int32)
    fault_remote = set_ends(jax.random.randint(splits[5], (OWNERS, OWNERS, FACES), 0, CX * CY * NZ), jax.random.fold_in(splits[5], 1), 0, (CX * CY * NZ) - 1).astype(jnp.int32)
    fault_count = draw_fault_count(jax.random.fold_in(splits[10], 71), 0)
    fault_mult = jnp.clip(jnp.exp(math.log(1.0) - 1.2039728 * jax.random.uniform(splits[7], (OWNERS, OWNERS, FACES), jnp.float32) ** block_levels(splits[7], (OWNERS, OWNERS, FACES), ((0, 128),), -0.2, 0.2)), 0.3, 1.0)
    low_bound = jnp.clip(jax.random.uniform(splits[8], (1,), jnp.float32, 0.02, 0.1), 0.02, 0.1)
    high_bound = jnp.clip(jax.random.uniform(splits[9], (1,), jnp.float32, 1.8, 2.0), 1.8, 2.0)
    return {"right_side": right_side, "permeability": permeability, "accumulation": accumulation, "active": active, "fault_local": fault_local, "fault_remote": fault_remote, "fault_count": fault_count, "fault_mult": fault_mult, "low_bound": low_bound, "high_bound": high_bound}


def harmonic(k_one, a_one, k_two, a_two, factor):
    return factor * (2.0 * (k_one * k_two)) / (k_one + k_two) * (a_one * a_two)


def global_index(owner, local):
    first = local // (CY * NZ)
    second = (local // NZ) % CY
    layer = local % NZ
    row = (owner // N_GY) * CX + first
    col = (owner % N_GY) * CY + second
    return ((row * NY + col) * NZ + layer).astype(jnp.int32)


def reference(right_side, permeability, accumulation, active, fault_local, fault_remote, fault_count, fault_mult, low_bound, high_bound):
    act = active.astype(jnp.float32)
    perm = permeability
    tx = harmonic(perm[:-1], act[:-1], perm[1:], act[1:], 1.0)
    ty = harmonic(perm[:, :-1], act[:, :-1], perm[:, 1:], act[:, 1:], 1.0)
    tz = harmonic(perm[:, :, :-1], act[:, :, :-1], perm[:, :, 1:], act[:, :, 1:], 0.8)
    owners = jnp.arange(NX // CX * (NY // CY), dtype=jnp.int32)
    first_end = global_index(owners[:, None, None], fault_local).reshape(-1)
    second_end = global_index(owners[None, :, None], fault_remote).reshape(-1)
    slots = jnp.arange(FACES, dtype=jnp.int32)
    valid = (slots[None, None, :] < fault_count[:, :, None]).astype(jnp.float32).reshape(-1)
    perm_flat = perm.reshape(-1)
    act_flat = act.reshape(-1)
    fault_trans = harmonic(perm_flat[first_end], act_flat[first_end], perm_flat[second_end], act_flat[second_end], 1.0) * fault_mult.reshape(-1) * valid
    diag_acc = jnp.where(active != 0, accumulation, jnp.float32(1.0))
    zero_pad = ((0, 0), (0, 0), (0, 0))

    def padded(values, axis, before):
        widths = list(zero_pad)
        widths[axis] = (1, 0) if before else (0, 1)
        return jnp.pad(values, widths)

    diagonal = diag_acc + padded(tx, 0, False) + padded(tx, 0, True)
    diagonal = diagonal + padded(ty, 1, False) + padded(ty, 1, True)
    diagonal = diagonal + padded(tz, 2, False) + padded(tz, 2, True)
    fault_diag = jnp.zeros(diagonal.size, jnp.float32).at[first_end].add(fault_trans).at[second_end].add(fault_trans)
    diagonal = diagonal + fault_diag.reshape(diagonal.shape)

    def operate(field):
        result = diag_acc * field
        flux = tx * (field[:-1] - field[1:])
        result = result + padded(flux, 0, False) - padded(flux, 0, True)
        flux = ty * (field[:, :-1] - field[:, 1:])
        result = result + padded(flux, 1, False) - padded(flux, 1, True)
        flux = tz * (field[:, :, :-1] - field[:, :, 1:])
        result = result + padded(flux, 2, False) - padded(flux, 2, True)
        flat = field.reshape(-1)
        fault_flux = fault_trans * (flat[first_end] - flat[second_end])
        extra = jnp.zeros(flat.size, jnp.float32).at[first_end].add(fault_flux).at[second_end].add(-fault_flux)
        return result + extra.reshape(field.shape)

    low = low_bound[0]
    high = high_bound[0]
    theta = (high + low) / 2.0
    delta = (high - low) / 2.0
    sigma = theta / delta
    rho = 1.0 / sigma
    correction = jnp.zeros_like(right_side)
    residual = right_side
    step = (residual / diagonal) / theta
    for count in range(ITERS):
        correction = correction + step
        residual = residual - operate(step)
        if count + 1 < ITERS:
            rho_new = 1.0 / (2.0 * sigma - rho)
            step = (rho_new * rho) * step + (2.0 * rho_new / delta) * (residual / diagonal)
            rho = rho_new
    return correction, residual
```

```python
import functools

import jax
import jax.numpy as jnp
from jax import lax
from jax.experimental import pallas as pl
from jax.experimental.pallas import tpu as pltpu
from jax.sharding import PartitionSpec as P

ITERS = 3
PEERS = 128
CHUNKS = 4
PER = PEERS // CHUNKS
LANES = 128
MESH = pl.DeviceIdType.MESH
F32 = jnp.float32
BF16 = jnp.bfloat16


def harmonic(k_one, k_two, factor):
    total = k_one + k_two
    safe = jnp.where(total > 0.0, total, 1.0)
    return factor * (2.0 * (k_one * k_two)) / safe


def split(values):
    head = values.astype(BF16)
    tail = (values - head.astype(F32)).astype(BF16)
    return head, tail


def offset_of(digit):
    return lax.rem(jnp.where(digit < 2, 2 - digit, digit + 1), 4)


def kernel(
    right_ref,
    perm_ref,
    acc_ref,
    active_ref,
    local_ref,
    remote_ref,
    mult_ref,
    count_ref,
    low_ref,
    high_ref,
    corr_ref,
    resid_ref,
    keff,
    diag_acc,
    diagonal,
    step_ref,
    trans,
    cell_row,
    lo_ref,
    hot_lanes,
    hot_rows,
    table,
    fault_trans,
    turned,
    send_a,
    recv_a,
    send_b,
    recv_b,
    send_p,
    recv_p,
    face_x_out,
    face_x_in,
    face_y_out,
    face_y_in,
    ssem,
    rsem,
    face_ssem,
    face_rsem,
):
    gx = lax.axis_index("gx")
    gy = lax.axis_index("gy")
    px, pz = gx // 4, lax.rem(gx, 4)
    py, pc = gy // 2, lax.rem(gy, 2)

    def peer(slot):
        dx = offset_of(slot // 32)
        dz = offset_of(lax.rem(slot // 8, 4))
        dy = offset_of(lax.rem(slot // 2, 4))
        dc = 1 - lax.rem(slot, 2)
        return (
            lax.rem(px + dx, 4) * 4 + lax.rem(pz + dz, 4),
            lax.rem(py + dy, 4) * 2 + lax.rem(pc + dc, 2),
        )

    def mirror(slot):
        def turn(digit):
            inner = jnp.logical_and(digit > 0, digit < 3)
            return jnp.where(inner, 3 - digit, digit)

        return (
            turn(slot // 32) * 32
            + turn(lax.rem(slot // 8, 4)) * 8
            + turn(lax.rem(slot // 2, 4)) * 2
            + lax.rem(slot, 2)
        )

    barrier = pltpu.get_barrier_semaphore()

    def greet(slot, carry):
        pl.semaphore_signal(barrier, inc=1, device_id=peer(slot), device_id_type=MESH)
        return carry

    lax.fori_loop(0, PEERS - 1, greet, 0)

    lane = lax.broadcasted_iota(jnp.int32, (1, LANES), 1)

    def order(slot, carry):
        ox, oy = peer(slot)
        owner = ox * 8 + oy
        cell_row[pl.ds(slot, 1), :] = local_ref[pl.ds(owner, 1), :]
        send_a[slot, 0:1, :] = remote_ref[pl.ds(owner, 1), :].astype(F32)
        mult = mult_ref[pl.ds(owner, 1), :]
        send_a[slot, 2:3, :] = jnp.where(lane < count_ref[0, owner], mult, 0.0)
        return carry

    lax.fori_loop(0, PEERS, order, 0)

    keff[...] = jnp.where(active_ref[...] != 0, perm_ref[...], 0.0)
    diag_acc[...] = jnp.where(active_ref[...] != 0, acc_ref[...], 1.0)

    def index_rows(kind):
        cells = cell_row[...]
        low = ((cells >> 12) * 2 + ((cells >> 8) & 1)) * 8 + ((cells >> 9) & 7)
        for chunk in range(CHUNKS):
            base = chunk * 2 * PER + kind * PER
            lo_ref[base : base + PER, :] = low[chunk * PER : (chunk + 1) * PER]
        turned[...] = jnp.transpose(cells & 255)
        down = lax.broadcasted_iota(jnp.int32, (256, LANES), 0)
        across = lax.broadcasted_iota(jnp.int32, (LANES, LANES), 1)

        def one(slot, carry):
            place = (slot // PER) * 2 * PER + kind * PER + lax.rem(slot, PER)
            start = pl.multiple_of(place * LANES, LANES)
            high = jnp.broadcast_to(cell_row[pl.ds(slot, 1), :] & 255, (256, LANES))
            hot_lanes[:, pl.ds(start, LANES)] = jnp.where(high == down, 1.0, 0.0).astype(BF16)
            pick = jnp.full((8, LANES), slot, jnp.int32)
            column = jnp.concatenate(
                [
                    jnp.take_along_axis(
                        turned[8 * i : 8 * i + 8, :], pick, axis=1, mode="promise_in_bounds"
                    )
                    for i in range(16)
                ],
                axis=0,
            )
            hot_rows[pl.ds(start, LANES), 0:128] = jnp.where(column == across, 1.0, 0.0).astype(BF16)
            hot_rows[pl.ds(start, LANES), 128:256] = jnp.where(
                column == across + 128, 1.0, 0.0
            ).astype(BF16)
            return carry

        lax.fori_loop(0, PEERS, one, 0)

    def set_table(values):
        for a in range(4):
            for h in range(2):
                row = (a * 2 + h) * 8
                head, tail = split(values[a, :, h * 256 : h * 256 + 256])
                table[row : row + 8, :] = head.astype(F32)
                table[64 + row : 72 + row, :] = tail.astype(F32)

    def gather(first, count, write):
        down = lax.broadcasted_iota(jnp.int32, (64, LANES), 0)
        start = pl.multiple_of(first * LANES, LANES)
        rows = table[...].astype(BF16)
        found = jnp.dot(
            rows, hot_lanes[:, pl.ds(start, count * LANES)], preferred_element_type=F32
        )
        for i in range(count):
            block = found[0:64, i * LANES : (i + 1) * LANES] + found[64:128, i * LANES : (i + 1) * LANES]
            mask = down == jnp.broadcast_to(lo_ref[pl.ds(first + i, 1), :], (64, LANES))
            write(i, jnp.sum(jnp.where(mask, block, 0.0), axis=0, keepdims=True))

    def scatter(first, count, values, total):
        down = lax.broadcasted_iota(jnp.int32, (64, LANES), 0)
        zero = jnp.zeros((64, LANES), BF16)
        heads, tails = [], []
        for i in range(count):
            head, tail = split(values(i))
            mask = down == jnp.broadcast_to(lo_ref[pl.ds(first + i, 1), :], (64, LANES))
            heads.append(jnp.where(mask, jnp.broadcast_to(head, (64, LANES)), zero))
            tails.append(jnp.where(mask, jnp.broadcast_to(tail, (64, LANES)), zero))
        spread = jnp.concatenate(
            [jnp.concatenate(heads, axis=1), jnp.concatenate(tails, axis=1)], axis=0
        )
        start = pl.multiple_of(first * LANES, LANES)
        return total + jnp.dot(
            spread, hot_rows[pl.ds(start, count * LANES), :], preferred_element_type=F32
        )

    def send(phase, chunk, source, target):
        def one(i, carry):
            slot = chunk * PER + i
            back = mirror(slot)
            pltpu.make_async_remote_copy(
                src_ref=source.at[slot],
                dst_ref=target.at[back],
                send_sem=ssem.at[phase],
                recv_sem=rsem.at[phase, back // PER],
                device_id=peer(slot),
                device_id_type=MESH,
            ).start()
            return carry

        lax.fori_loop(0, jnp.where(chunk == CHUNKS - 1, PER - 1, PER), one, 0)

    def wait_chunk(phase, chunk, target):
        count = PER - 1 if chunk == CHUNKS - 1 else PER
        block = target.at[pl.ds(chunk * PER, count)]
        pltpu.make_async_copy(block, block, rsem.at[phase, chunk]).wait()

    def wait_sent(phase, source):
        block = source.at[pl.ds(0, PEERS - 1)]
        pltpu.make_async_copy(block, block, ssem.at[phase]).wait()

    def face_copies(phase):
        west = (lax.rem(gx + 15, 16), gy)
        east = (lax.rem(gx + 1, 16), gy)
        south = (gx, lax.rem(gy + 7, 8))
        north = (gx, lax.rem(gy + 1, 8))
        plan = (
            (face_x_out, face_x_in, 0, 1, west),
            (face_x_out, face_x_in, 1, 0, east),
            (face_y_out, face_y_in, 0, 1, south),
            (face_y_out, face_y_in, 1, 0, north),
        )
        copies = []
        for number, (out, into, side, other, device) in enumerate(plan):
            copies.append(
                pltpu.make_async_remote_copy(
                    src_ref=out.at[phase, side],
                    dst_ref=into.at[phase, other],
                    send_sem=face_ssem.at[phase, number],
                    recv_sem=face_rsem.at[phase, number],
                    device_id=device,
                    device_id_type=MESH,
                )
            )
        return copies

    def send_faces(phase, values):
        face_x_out[phase, 0] = values[0]
        face_x_out[phase, 1] = values[3]
        for a in range(4):
            face_y_out[phase, 0, a : a + 1, :] = values[a, 0:1, :]
            face_y_out[phase, 1, a : a + 1, :] = values[a, 7:8, :]
        for copy in face_copies(phase):
            copy.start()

    def beside(values, phase, a):
        plane = values[a]
        east = values[a + 1] if a < 3 else face_x_in[phase, 1]
        west = values[a - 1] if a > 0 else face_x_in[phase, 0]
        north = jnp.concatenate([plane[1:8], face_y_in[phase, 1, a : a + 1, :]], axis=0)
        south = jnp.concatenate([face_y_in[phase, 0, a : a + 1, :], plane[0:7]], axis=0)
        above = pltpu.roll(plane, 511, 1)
        below = pltpu.roll(plane, 1, 1)
        return plane, (east, west, north, south, above, below)

    index_rows(0)
    set_table(keff)

    for chunk in range(CHUNKS):

        def put_k(i, row, chunk=chunk):
            send_a[chunk * PER + i, 1:2, :] = row

        gather(chunk * 2 * PER, PER, put_k)

    pl.semaphore_wait(barrier, PEERS - 1)

    for chunk in range(CHUNKS):
        send(0, chunk, send_a, recv_a)
    send_faces(0, keff)
    recv_a[PEERS - 1] = send_a[PEERS - 1]
    for chunk in range(CHUNKS):
        wait_chunk(0, chunk, recv_a)
        for i in range(PER):
            slot = chunk * PER + i
            cell_row[slot : slot + 1, :] = recv_a[slot, 0:1, :].astype(jnp.int32)
    index_rows(1)

    for chunk in range(CHUNKS):

        def put_k(i, row, chunk=chunk):
            send_b[chunk * PER + i, 0:1, :] = row

        gather(chunk * 2 * PER + PER, PER, put_k)
        send(1, chunk, send_b, recv_b)
    recv_b[PEERS - 1] = send_b[PEERS - 1]
    for copy in face_copies(0):
        copy.wait_recv()

    at_x = (gx > 0, gx < 15)
    at_y = (gy > 0, gy < 7)
    for side in range(2):
        face_x_in[0, side] = jnp.where(at_x[side], face_x_in[0, side], 0.0)
        face_y_in[0, side] = jnp.where(at_y[side], face_y_in[0, side], 0.0)
    layer = lax.broadcasted_iota(jnp.int32, (8, 512), 1)
    for a in range(4):
        plane, others = beside(keff, 0, a)
        amount = diag_acc[a]
        for side in range(6):
            other = others[side]
            if side == 4:
                other = jnp.where(layer == 511, 0.0, other)
            if side == 5:
                other = jnp.where(layer == 0, 0.0, other)
            one = harmonic(plane, other, 0.8 if side >= 4 else 1.0)
            trans[side, a] = one
            amount = amount + one
        diagonal[a] = amount

    total = jnp.zeros((128, 256), F32)
    for chunk in range(CHUNKS):
        first = chunk * 2 * PER

        def asked(i, chunk=chunk, first=first):
            slot = chunk * PER + i
            value = (
                harmonic(recv_a[slot, 1:2, :], send_b[slot, 0:1, :], 1.0) * recv_a[slot, 2:3, :]
            )
            fault_trans[first + PER + i : first + PER + i + 1, :] = value
            return value

        total = scatter(first + PER, PER, asked, total)
    for chunk in range(CHUNKS):
        wait_chunk(1, chunk, recv_b)
        first = chunk * 2 * PER

        def owned(i, chunk=chunk, first=first):
            slot = chunk * PER + i
            value = (
                harmonic(send_a[slot, 1:2, :], recv_b[slot, 0:1, :], 1.0) * send_a[slot, 2:3, :]
            )
            fault_trans[first + i : first + i + 1, :] = value
            return value

        total = scatter(first, PER, owned, total)

    def place(total, a):
        halves = [
            total[(a * 2 + h) * 8 : (a * 2 + h) * 8 + 8, :]
            + total[64 + (a * 2 + h) * 8 : 64 + (a * 2 + h) * 8 + 8, :]
            for h in range(2)
        ]
        return jnp.concatenate(halves, axis=1)

    low = jnp.full((8, 512), low_ref[0], F32)
    high = jnp.full((8, 512), high_ref[0], F32)
    theta = (high + low) / 2.0
    delta = (high - low) / 2.0
    sigma = theta / delta
    for a in range(4):
        diagonal[a] = diagonal[a] + place(total, a)
        resid_ref[a] = right_ref[a]
        step_ref[a] = right_ref[a] / diagonal[a] / theta
        corr_ref[a] = jnp.zeros((8, 512), F32)

    def iteration(count, rho):
        phase = count + 2
        face_phase = count + 1
        send_faces(face_phase, step_ref)
        set_table(step_ref)
        source, target = send_p.at[count], recv_p.at[count]

        def ask(chunk, carry):
            for kind in range(2):

                def put_p(i, row, kind=kind):
                    source[chunk * PER + i, kind : kind + 1, :] = row

                gather(chunk * 2 * PER + kind * PER, PER, put_p)
            send(phase, chunk, source, target)
            return carry

        lax.fori_loop(0, CHUNKS, ask, 0)
        target[PEERS - 1] = source[PEERS - 1]
        total = jnp.zeros((128, 256), F32)
        for chunk in range(CHUNKS):
            wait_chunk(phase, chunk, target)
            first = chunk * 2 * PER

            def flux(i, chunk=chunk, first=first):
                slot, kind = chunk * PER + i % PER, i // PER
                return fault_trans[first + i : first + i + 1, :] * (
                    source[slot, kind : kind + 1, :] - target[slot, 1 - kind : 2 - kind, :]
                )

            total = scatter(first, 2 * PER, flux, total)
        for copy in face_copies(face_phase):
            copy.wait_recv()
        rho_new = 1.0 / (2.0 * sigma - rho)
        news = []
        for a in range(4):
            plane, others = beside(step_ref, face_phase, a)
            result = diag_acc[a] * plane
            for side in range(6):
                result = result + trans[side, a] * (plane - others[side])
            corr_ref[a] = corr_ref[a] + plane
            resid = resid_ref[a] - (result + place(total, a))
            resid_ref[a] = resid
            news.append(rho_new * rho * plane + 2.0 * rho_new / delta * (resid / diagonal[a]))
        for a in range(4):
            step_ref[a] = news[a]
        wait_sent(phase, source)
        for copy in face_copies(face_phase):
            copy.wait_send()
        return rho_new

    lax.fori_loop(0, ITERS, iteration, 1.0 / sigma)
    wait_sent(0, send_a)
    wait_sent(1, send_b)
    for copy in face_copies(0):
        copy.wait_send()


def on_device(
    right_side,
    permeability,
    accumulation,
    active,
    fault_local,
    fault_remote,
    fault_count,
    fault_mult,
    low_bound,
    high_bound,
):
    shape = right_side.shape
    vmem = pl.BlockSpec(memory_space=pltpu.VMEM)
    smem = pl.BlockSpec(memory_space=pltpu.SMEM)
    rows = 2 * PEERS
    cells = pltpu.VMEM(shape, F32)
    return tuple(
        pl.pallas_call(
            kernel,
            out_shape=[jax.ShapeDtypeStruct(shape, F32)] * 2,
            in_specs=[vmem] * 7 + [smem] * 3,
            out_specs=[vmem] * 2,
            scratch_shapes=[
                cells,
                cells,
                cells,
                cells,
                pltpu.VMEM((6,) + shape, F32),
                pltpu.VMEM((PEERS, LANES), jnp.int32),
                pltpu.VMEM((rows, LANES), jnp.int32),
                pltpu.VMEM((256, rows * LANES), BF16),
                pltpu.VMEM((rows * LANES, 256), BF16),
                pltpu.VMEM((128, 256), F32),
                pltpu.VMEM((rows, LANES), F32),
                pltpu.VMEM((LANES, LANES), jnp.int32),
                pltpu.VMEM((PEERS, 4, LANES), F32),
                pltpu.VMEM((PEERS, 4, LANES), F32),
                pltpu.VMEM((PEERS, 1, LANES), F32),
                pltpu.VMEM((PEERS, 1, LANES), F32),
                pltpu.VMEM((ITERS, PEERS, 2, LANES), F32),
                pltpu.VMEM((ITERS, PEERS, 2, LANES), F32),
                pltpu.VMEM((ITERS + 1, 2, 8, 512), F32),
                pltpu.VMEM((ITERS + 1, 2, 8, 512), F32),
                pltpu.VMEM((ITERS + 1, 2, 4, 512), F32),
                pltpu.VMEM((ITERS + 1, 2, 4, 512), F32),
                pltpu.SemaphoreType.DMA((ITERS + 2,)),
                pltpu.SemaphoreType.DMA((ITERS + 2, CHUNKS)),
                pltpu.SemaphoreType.DMA((ITERS + 1, 4)),
                pltpu.SemaphoreType.DMA((ITERS + 1, 4)),
            ],
            compiler_params=pltpu.CompilerParams(
                collective_id=0, has_side_effects=True, vmem_limit_bytes=56 * 2**20
            ),
        )(
            right_side,
            permeability,
            accumulation,
            active,
            fault_local.reshape(PEERS, LANES),
            fault_remote.reshape(PEERS, LANES),
            fault_mult.reshape(PEERS, LANES),
            fault_count,
            low_bound,
            high_bound,
        )
    )


def solution(mesh):
    in_specs = (
        P("gx", "gy", None),
        P("gx", "gy", None),
        P("gx", "gy", None),
        P("gx", "gy", None),
        P(("gx", "gy"), None, None),
        P(("gx", "gy"), None, None),
        P(("gx", "gy"), None),
        P(("gx", "gy"), None, None),
        P(),
        P(),
    )
    out_specs = (P("gx", "gy", None), P("gx", "gy", None))
    return jax.shard_map(
        on_device, mesh=mesh, in_specs=in_specs, out_specs=out_specs, check_vma=False
    )
```

```python
import functools

import jax
import jax.numpy as jnp
from jax import lax
from jax.experimental import pallas as pl
from jax.experimental.pallas import tpu as pltpu
from jax.sharding import PartitionSpec as P

ITERS = 3
PEERS = 128
CHUNKS = 4
PER = PEERS // CHUNKS
LANES = 128
MESH = pl.DeviceIdType.MESH
F32 = jnp.float32
BF16 = jnp.bfloat16


def harmonic(k_one, k_two, factor):
    total = k_one + k_two
    safe = jnp.where(total > 0.0, total, 1.0)
    return factor * (2.0 * (k_one * k_two)) / safe


def split(values):
    head = values.astype(BF16)
    tail = (values - head.astype(F32)).astype(BF16)
    return head, tail


def slot_plan():
    def hops(offset):
        return sum(min(d, 4 - d) for d in offset[:3])

    def opposite(offset):
        return tuple(-d % 4 for d in offset[:3]) + (offset[3],)

    offsets = [(x, z, y, c) for x in range(4) for z in range(4) for y in range(4) for c in range(2)]

    def rank(offset):
        pair = min(offset[:3], opposite(offset)[:3])
        alone = offset[:3] == opposite(offset)[:3]
        first = alone if hops(offset) == 2 else not alone
        return (-hops(offset), first, pair, offset[:3], 1 - offset[3])

    offsets.sort(key=rank)
    return offsets, [offsets.index(opposite(offset)) for offset in offsets]


OFFSETS, MIRROR = slot_plan()


def kernel(
    right_ref,
    perm_ref,
    acc_ref,
    active_ref,
    local_ref,
    remote_ref,
    mult_ref,
    count_ref,
    low_ref,
    high_ref,
    corr_ref,
    resid_ref,
    keff,
    diag_acc,
    diagonal,
    step_ref,
    trans,
    cell_row,
    lo_ref,
    hot_lanes,
    hot_rows,
    table,
    fault_trans,
    turned,
    grid_part,
    send_i,
    recv_i,
    send_a,
    recv_a,
    send_b,
    recv_b,
    send_p,
    recv_p,
    face_x_out,
    face_x_in,
    face_y_out,
    face_y_in,
    ssem,
    rsem,
    face_ssem,
    face_rsem,
):
    gx = lax.axis_index("gx")
    gy = lax.axis_index("gy")
    at_x = [lax.rem(gx // 4 + d, 4) * 4 for d in range(4)]
    at_z = [lax.rem(lax.rem(gx, 4) + d, 4) for d in range(4)]
    at_y = [lax.rem(gy // 2 + d, 4) * 2 for d in range(4)]
    at_c = [lax.rem(lax.rem(gy, 2) + d, 2) for d in range(2)]

    def peer(slot):
        dx, dz, dy, dc = OFFSETS[slot]
        return (at_x[dx] + at_z[dz], at_y[dy] + at_c[dc])

    barrier = pltpu.get_barrier_semaphore()

    for slot in range(PEERS - 1):
        pl.semaphore_signal(barrier, inc=1, device_id=peer(slot), device_id_type=MESH)

    lane = lax.broadcasted_iota(jnp.int32, (1, LANES), 1)
    for slot in range(PEERS):
        ox, oy = peer(slot)
        owner = ox * 8 + oy
        cell_row[slot : slot + 1, :] = local_ref[pl.ds(owner, 1), :]
        send_i[slot, 0:1, :] = remote_ref[pl.ds(owner, 1), :]
        mult = mult_ref[pl.ds(owner, 1), :]
        send_a[slot, 1:2, :] = jnp.where(lane < count_ref[0, owner], mult, 0.0)

    keff[...] = jnp.where(active_ref[...] != 0, perm_ref[...], 0.0)
    diag_acc[...] = jnp.where(active_ref[...] != 0, acc_ref[...], 1.0)

    down = lax.broadcasted_iota(jnp.int32, (256, LANES), 0)
    across = lax.broadcasted_iota(jnp.int32, (LANES, LANES), 1)

    def index_lanes(kind, chunk):
        cells = cell_row[chunk * PER : (chunk + 1) * PER, :]
        base = chunk * 2 * PER + kind * PER
        lo_ref[base : base + PER, :] = (
            ((cells >> 12) * 2 + ((cells >> 8) & 1)) * 8 + ((cells >> 9) & 7)
        )

        def some(step, carry):
            for i in range(8):
                row = chunk * PER + step * 8 + i
                start = pl.multiple_of((base + step * 8 + i) * LANES, LANES)
                high = jnp.broadcast_to(cell_row[pl.ds(row, 1), :] & 255, (256, LANES))
                hot_lanes[:, pl.ds(start, LANES)] = jnp.where(high == down, 1.0, 0.0).astype(BF16)
            return carry

        lax.fori_loop(0, PER // 8, some, 0)

    def index_rows(kind):
        turned[...] = jnp.transpose(cell_row[...] & 255)

        def some(step, carry):
            for i in range(4):
                slot = step * 4 + i
                pick = jnp.full((8, LANES), slot, jnp.int32)
                column = jnp.concatenate(
                    [
                        jnp.take_along_axis(
                            turned[8 * j : 8 * j + 8, :], pick, axis=1, mode="promise_in_bounds"
                        )
                        for j in range(16)
                    ],
                    axis=0,
                )
                place = (slot // PER) * 2 * PER + kind * PER + lax.rem(slot, PER)
                start = pl.multiple_of(place * LANES, LANES)
                for half in range(2):
                    hot_rows[pl.ds(start, LANES), half * 128 : half * 128 + 128] = jnp.where(
                        column == across + half * 128, 1.0, 0.0
                    ).astype(BF16)
            return carry

        lax.fori_loop(0, PEERS // 4, some, 0)

    def set_table(values):
        for a in range(4):
            for h in range(2):
                row = (a * 2 + h) * 8
                head, tail = split(values[a, :, h * 256 : h * 256 + 256])
                table[row : row + 8, :] = head.astype(F32)
                table[64 + row : 72 + row, :] = tail.astype(F32)

    def gather(first, count, write):
        down = lax.broadcasted_iota(jnp.int32, (64, LANES), 0)
        start = pl.multiple_of(first * LANES, LANES)
        rows = table[...].astype(BF16)
        found = jnp.dot(
            rows, hot_lanes[:, pl.ds(start, count * LANES)], preferred_element_type=F32
        )
        for i in range(count):
            block = found[0:64, i * LANES : (i + 1) * LANES] + found[64:128, i * LANES : (i + 1) * LANES]
            mask = down == jnp.broadcast_to(lo_ref[pl.ds(first + i, 1), :], (64, LANES))
            write(i, jnp.sum(jnp.where(mask, block, 0.0), axis=0, keepdims=True))

    def scatter(first, count, values, total):
        down = lax.broadcasted_iota(jnp.int32, (64, LANES), 0)
        zero = jnp.zeros((64, LANES), BF16)
        heads, tails = [], []
        for i in range(count):
            head, tail = split(values(i))
            mask = down == jnp.broadcast_to(lo_ref[pl.ds(first + i, 1), :], (64, LANES))
            heads.append(jnp.where(mask, jnp.broadcast_to(head, (64, LANES)), zero))
            tails.append(jnp.where(mask, jnp.broadcast_to(tail, (64, LANES)), zero))
        spread = jnp.concatenate(
            [jnp.concatenate(heads, axis=1), jnp.concatenate(tails, axis=1)], axis=0
        )
        start = pl.multiple_of(first * LANES, LANES)
        return total + jnp.dot(
            spread, hot_rows[pl.ds(start, count * LANES), :], preferred_element_type=F32
        )

    def send(phase, chunk, source, target):
        for slot in range(chunk * PER, (chunk + 1) * PER):
            if slot < PEERS - 1:
                back = MIRROR[slot]
                pltpu.make_async_remote_copy(
                    src_ref=source.at[slot],
                    dst_ref=target.at[back],
                    send_sem=ssem.at[phase],
                    recv_sem=rsem.at[phase, back // PER],
                    device_id=peer(slot),
                    device_id_type=MESH,
                ).start()

    def wait_chunk(phase, chunk, target):
        count = PER - 1 if chunk == CHUNKS - 1 else PER
        block = target.at[pl.ds(chunk * PER, count)]
        pltpu.make_async_copy(block, block, rsem.at[phase, chunk]).wait()

    def wait_sent(phase, source):
        block = source.at[pl.ds(0, PEERS - 1)]
        pltpu.make_async_copy(block, block, ssem.at[phase]).wait()

    def face_copies(phase):
        west = (lax.rem(gx + 15, 16), gy)
        east = (lax.rem(gx + 1, 16), gy)
        south = (gx, lax.rem(gy + 7, 8))
        north = (gx, lax.rem(gy + 1, 8))
        plan = (
            (face_x_out, face_x_in, 0, 1, west),
            (face_x_out, face_x_in, 1, 0, east),
            (face_y_out, face_y_in, 0, 1, south),
            (face_y_out, face_y_in, 1, 0, north),
        )
        copies = []
        for number, (out, into, side, other, device) in enumerate(plan):
            copies.append(
                pltpu.make_async_remote_copy(
                    src_ref=out.at[phase, side],
                    dst_ref=into.at[phase, other],
                    send_sem=face_ssem.at[phase, number],
                    recv_sem=face_rsem.at[phase, number],
                    device_id=device,
                    device_id_type=MESH,
                )
            )
        return copies

    def send_faces(phase, values):
        face_x_out[phase, 0] = values[0]
        face_x_out[phase, 1] = values[3]
        for a in range(4):
            face_y_out[phase, 0, a : a + 1, :] = values[a, 0:1, :]
            face_y_out[phase, 1, a : a + 1, :] = values[a, 7:8, :]
        for copy in face_copies(phase):
            copy.start()

    def beside(values, phase, a):
        plane = values[a]
        east = values[a + 1] if a < 3 else face_x_in[phase, 1]
        west = values[a - 1] if a > 0 else face_x_in[phase, 0]
        north = jnp.concatenate([plane[1:8], face_y_in[phase, 1, a : a + 1, :]], axis=0)
        south = jnp.concatenate([face_y_in[phase, 0, a : a + 1, :], plane[0:7]], axis=0)
        above = pltpu.roll(plane, 511, 1)
        below = pltpu.roll(plane, 1, 1)
        return plane, (east, west, north, south, above, below)

    set_table(keff)
    for chunk in range(CHUNKS):

        def put_k(i, row, chunk=chunk):
            send_a[chunk * PER + i, 0:1, :] = row

        index_lanes(0, chunk)
        gather(chunk * 2 * PER, PER, put_k)
    index_rows(0)

    pl.semaphore_wait(barrier, PEERS - 1)

    for chunk in range(CHUNKS):
        send(0, chunk, send_i, recv_i)
    send_faces(0, keff)
    for chunk in range(CHUNKS):
        send(1, chunk, send_a, recv_a)
    recv_i[PEERS - 1] = send_i[PEERS - 1]
    recv_a[PEERS - 1] = send_a[PEERS - 1]

    for chunk in range(CHUNKS):
        wait_chunk(0, chunk, recv_i)
        for i in range(PER):
            slot = chunk * PER + i
            cell_row[slot : slot + 1, :] = recv_i[slot, 0:1, :]
        index_lanes(1, chunk)

        def put_k(i, row, chunk=chunk):
            send_b[chunk * PER + i, 0:1, :] = row

        gather(chunk * 2 * PER + PER, PER, put_k)
        send(2, chunk, send_b, recv_b)
    recv_b[PEERS - 1] = send_b[PEERS - 1]
    index_rows(1)
    for copy in face_copies(0):
        copy.wait_recv()

    inside_x = (gx > 0, gx < 15)
    inside_y = (gy > 0, gy < 7)
    for side in range(2):
        face_x_in[0, side] = jnp.where(inside_x[side], face_x_in[0, side], 0.0)
        face_y_in[0, side] = jnp.where(inside_y[side], face_y_in[0, side], 0.0)
    layer = lax.broadcasted_iota(jnp.int32, (8, 512), 1)
    for a in range(4):
        plane, others = beside(keff, 0, a)
        amount = diag_acc[a]
        for side in range(6):
            other = others[side]
            if side == 4:
                other = jnp.where(layer == 511, 0.0, other)
            if side == 5:
                other = jnp.where(layer == 0, 0.0, other)
            one = harmonic(plane, other, 0.8 if side >= 4 else 1.0)
            trans[side, a] = one
            amount = amount + one
        diagonal[a] = amount

    total = jnp.zeros((128, 256), F32)
    for chunk in range(CHUNKS):
        wait_chunk(1, chunk, recv_a)
        first = chunk * 2 * PER

        def asked(i, chunk=chunk, first=first):
            slot = chunk * PER + i
            value = (
                harmonic(recv_a[slot, 0:1, :], send_b[slot, 0:1, :], 1.0) * recv_a[slot, 1:2, :]
            )
            fault_trans[first + PER + i : first + PER + i + 1, :] = value
            return value

        total = scatter(first + PER, PER, asked, total)
    for chunk in range(CHUNKS):
        wait_chunk(2, chunk, recv_b)
        first = chunk * 2 * PER

        def owned(i, chunk=chunk, first=first):
            slot = chunk * PER + i
            value = (
                harmonic(send_a[slot, 0:1, :], recv_b[slot, 0:1, :], 1.0) * send_a[slot, 1:2, :]
            )
            fault_trans[first + i : first + i + 1, :] = value
            return value

        total = scatter(first, PER, owned, total)

    def place(total, a):
        halves = [
            total[(a * 2 + h) * 8 : (a * 2 + h) * 8 + 8, :]
            + total[64 + (a * 2 + h) * 8 : 64 + (a * 2 + h) * 8 + 8, :]
            for h in range(2)
        ]
        return jnp.concatenate(halves, axis=1)

    low = jnp.broadcast_to(low_ref[...], (8, 512))
    high = jnp.broadcast_to(high_ref[...], (8, 512))
    theta = (high + low) / 2.0
    delta = (high - low) / 2.0
    sigma = theta / delta
    for a in range(4):
        diagonal[a] = diagonal[a] + place(total, a)
        resid_ref[a] = right_ref[a]
        step_ref[a] = right_ref[a] / diagonal[a] / theta
        corr_ref[a] = jnp.zeros((8, 512), F32)

    def iteration(count, rho):
        phase = count + 3
        face_phase = count + 1
        send_faces(face_phase, step_ref)
        set_table(step_ref)
        source, target = send_p.at[count], recv_p.at[count]
        for chunk in range(CHUNKS):
            for kind in range(2):

                def put_p(i, row, chunk=chunk, kind=kind):
                    source[chunk * PER + i, kind : kind + 1, :] = row

                gather(chunk * 2 * PER + kind * PER, PER, put_p)
            send(phase, chunk, source, target)
        target[PEERS - 1] = source[PEERS - 1]
        for copy in face_copies(face_phase):
            copy.wait_recv()
        for a in range(4):
            plane, others = beside(step_ref, face_phase, a)
            result = diag_acc[a] * plane
            for side in range(6):
                result = result + trans[side, a] * (plane - others[side])
            corr_ref[a] = corr_ref[a] + plane
            grid_part[a] = result
        total = jnp.zeros((128, 256), F32)
        for chunk in range(CHUNKS):
            wait_chunk(phase, chunk, target)
            first = chunk * 2 * PER

            def flux(i, chunk=chunk, first=first):
                slot, kind = chunk * PER + i % PER, i // PER
                return fault_trans[first + i : first + i + 1, :] * (
                    source[slot, kind : kind + 1, :] - target[slot, 1 - kind : 2 - kind, :]
                )

            total = scatter(first, 2 * PER, flux, total)
        rho_new = 1.0 / (2.0 * sigma - rho)
        for a in range(4):
            resid = resid_ref[a] - (grid_part[a] + place(total, a))
            resid_ref[a] = resid
            step_ref[a] = rho_new * rho * step_ref[a] + 2.0 * rho_new / delta * (resid / diagonal[a])
        return rho_new

    lax.fori_loop(0, ITERS, iteration, 1.0 / sigma)
    sent = [send_i, send_a, send_b] + [send_p.at[count] for count in range(ITERS)]
    for phase, source in enumerate(sent):
        wait_sent(phase, source)
    for phase in range(ITERS + 1):
        for copy in face_copies(phase):
            copy.wait_send()


def on_device(
    right_side,
    permeability,
    accumulation,
    active,
    fault_local,
    fault_remote,
    fault_count,
    fault_mult,
    low_bound,
    high_bound,
):
    shape = right_side.shape
    vmem = pl.BlockSpec(memory_space=pltpu.VMEM)
    smem = pl.BlockSpec(memory_space=pltpu.SMEM)
    rows = 2 * PEERS
    cells = pltpu.VMEM(shape, F32)
    return tuple(
        pl.pallas_call(
            kernel,
            out_shape=[jax.ShapeDtypeStruct(shape, F32)] * 2,
            in_specs=[vmem] * 7 + [smem] + [vmem] * 2,
            out_specs=[vmem] * 2,
            scratch_shapes=[
                cells,
                cells,
                cells,
                cells,
                pltpu.VMEM((6,) + shape, F32),
                pltpu.VMEM((PEERS, LANES), jnp.int32),
                pltpu.VMEM((rows, LANES), jnp.int32),
                pltpu.VMEM((256, rows * LANES), BF16),
                pltpu.VMEM((rows * LANES, 256), BF16),
                pltpu.VMEM((128, 256), F32),
                pltpu.VMEM((rows, LANES), F32),
                pltpu.VMEM((LANES, LANES), jnp.int32),
                cells,
                pltpu.VMEM((PEERS, 1, LANES), jnp.int32),
                pltpu.VMEM((PEERS, 1, LANES), jnp.int32),
                pltpu.VMEM((PEERS, 2, LANES), F32),
                pltpu.VMEM((PEERS, 2, LANES), F32),
                pltpu.VMEM((PEERS, 1, LANES), F32),
                pltpu.VMEM((PEERS, 1, LANES), F32),
                pltpu.VMEM((ITERS, PEERS, 2, LANES), F32),
                pltpu.VMEM((ITERS, PEERS, 2, LANES), F32),
                pltpu.VMEM((ITERS + 1, 2, 8, 512), F32),
                pltpu.VMEM((ITERS + 1, 2, 8, 512), F32),
                pltpu.VMEM((ITERS + 1, 2, 4, 512), F32),
                pltpu.VMEM((ITERS + 1, 2, 4, 512), F32),
                pltpu.SemaphoreType.DMA((ITERS + 3,)),
                pltpu.SemaphoreType.DMA((ITERS + 3, CHUNKS)),
                pltpu.SemaphoreType.DMA((ITERS + 1, 4)),
                pltpu.SemaphoreType.DMA((ITERS + 1, 4)),
            ],
            compiler_params=pltpu.CompilerParams(
                collective_id=0, has_side_effects=True, vmem_limit_bytes=56 * 2**20
            ),
        )(
            right_side,
            permeability,
            accumulation,
            active,
            fault_local.reshape(PEERS, LANES),
            fault_remote.reshape(PEERS, LANES),
            fault_mult.reshape(PEERS, LANES),
            fault_count,
            low_bound.reshape(1, 1),
            high_bound.reshape(1, 1),
        )
    )


def solution(mesh):
    in_specs = (
        P("gx", "gy", None),
        P("gx", "gy", None),
        P("gx", "gy", None),
        P("gx", "gy", None),
        P(("gx", "gy"), None, None),
        P(("gx", "gy"), None, None),
        P(("gx", "gy"), None),
        P(("gx", "gy"), None, None),
        P(),
        P(),
    )
    out_specs = (P("gx", "gy", None), P("gx", "gy", None))
    return jax.shard_map(
        on_device, mesh=mesh, in_specs=in_specs, out_specs=out_specs, check_vma=False
    )
```

```python
import functools

import jax
import jax.numpy as jnp
from jax import lax
from jax.experimental import pallas as pl
from jax.experimental.pallas import tpu as pltpu
from jax.sharding import PartitionSpec as P

ITERS = 3
PEERS = 128
CHUNKS = 4
PER = PEERS // CHUNKS
LANES = 128
MESH = pl.DeviceIdType.MESH
F32 = jnp.float32
BF16 = jnp.bfloat16


def harmonic(k_one, k_two, factor):
    total = k_one + k_two
    safe = jnp.where(total > 0.0, total, 1.0)
    return factor * (2.0 * (k_one * k_two)) / safe


def split(values):
    head = values.astype(BF16)
    tail = (values - head.astype(F32)).astype(BF16)
    return head, tail


def slot_plan():
    def hops(offset):
        return sum(min(d, 4 - d) for d in offset[:2])

    offsets = [(z, y, c) for z in range(4) for y in range(4) for c in range(2)]
    offsets.sort(key=lambda offset: (-hops(offset), offset[0], offset[1], 1 - offset[2]))
    mirror = [offsets.index((-z % 4, -y % 4, c)) for z, y, c in offsets]
    return offsets, mirror


OFFSETS, MIRROR = slot_plan()


def kernel(
    right_ref,
    perm_ref,
    acc_ref,
    active_ref,
    local_ref,
    remote_ref,
    mult_ref,
    count_ref,
    low_ref,
    high_ref,
    corr_ref,
    resid_ref,
    keff,
    diag_acc,
    diagonal,
    step_ref,
    trans,
    cell_row,
    lo_ref,
    hot_lanes,
    hot_rows,
    table,
    fault_trans,
    turned,
    grid_part,
    send_a,
    recv_a,
    send_b,
    recv_b,
    send_p,
    recv_p,
    face_x_out,
    face_x_in,
    face_y_out,
    face_y_in,
    ssem,
    rsem,
    face_ssem,
    face_rsem,
):
    gx = lax.axis_index("gx")
    gy = lax.axis_index("gy")
    at_z = [lax.rem(lax.rem(gx, 4) + d, 4) for d in range(4)]
    at_y = [lax.rem(gy // 2 + d, 4) * 2 for d in range(4)]
    at_c = [lax.rem(lax.rem(gy, 2) + d, 2) for d in range(2)]

    def row_of(chunk):
        offset = lax.rem(jnp.where(chunk < 2, 2 - chunk, chunk + 1), 4)
        return lax.rem(gx // 4 + offset, 4) * 4

    def peer(base, i):
        dz, dy, dc = OFFSETS[i]
        return (base + at_z[dz], at_y[dy] + at_c[dc])

    def each(body):
        def one(chunk, carry):
            body(chunk)
            return carry

        lax.fori_loop(0, CHUNKS, one, 0)

    barrier = pltpu.get_barrier_semaphore()

    @each
    def greet(chunk):
        base = row_of(chunk)
        for i in range(PER):

            def signal(i=i):
                pl.semaphore_signal(barrier, inc=1, device_id=peer(base, i), device_id_type=MESH)

            if i < PER - 1:
                signal()
            else:
                pl.when(chunk < CHUNKS - 1)(signal)

    lane = lax.broadcasted_iota(jnp.int32, (1, LANES), 1)

    @each
    def order(chunk):
        base = row_of(chunk)
        for i in range(PER):
            slot = chunk * PER + i
            ox, oy = peer(base, i)
            owner = ox * 8 + oy
            cell_row[pl.ds(slot, 1), :] = local_ref[pl.ds(owner, 1), :]
            send_a[slot, 2:3, :] = remote_ref[pl.ds(owner, 1), :].astype(F32)
            mult = mult_ref[pl.ds(owner, 1), :]
            send_a[slot, 1:2, :] = jnp.where(lane < count_ref[0, owner], mult, 0.0)

    keff[...] = jnp.where(active_ref[...] != 0, perm_ref[...], 0.0)
    diag_acc[...] = jnp.where(active_ref[...] != 0, acc_ref[...], 1.0)

    down = lax.broadcasted_iota(jnp.int32, (256, LANES), 0)
    across = lax.broadcasted_iota(jnp.int32, (LANES, LANES), 1)

    def index_lanes(kind, chunk):
        cells = cell_row[pl.ds(pl.multiple_of(chunk * PER, PER), PER), :]
        base = pl.multiple_of(chunk * 2 * PER + kind * PER, PER)
        lo_ref[pl.ds(base, PER), :] = (
            ((cells >> 12) * 2 + ((cells >> 8) & 1)) * 8 + ((cells >> 9) & 7)
        )

        def some(step, carry):
            for i in range(8):
                row = chunk * PER + step * 8 + i
                start = pl.multiple_of((base + step * 8 + i) * LANES, LANES)
                high = jnp.broadcast_to(cell_row[pl.ds(row, 1), :] & 255, (256, LANES))
                hot_lanes[:, pl.ds(start, LANES)] = jnp.where(high == down, 1.0, 0.0).astype(BF16)
            return carry

        lax.fori_loop(0, PER // 8, some, 0)

    def index_rows(kind):
        turned[...] = jnp.transpose(cell_row[...] & 255)

        def some(step, carry):
            shifted = pltpu.roll(turned[...], lax.rem(LANES - step * 16, LANES), 1)
            for i in range(16):
                slot = step * 16 + i
                column = jnp.broadcast_to(shifted[:, i : i + 1], (LANES, LANES))
                place = (slot // PER) * 2 * PER + kind * PER + lax.rem(slot, PER)
                start = pl.multiple_of(place * LANES, LANES)
                for half in range(2):
                    hot_rows[pl.ds(start, LANES), half * 128 : half * 128 + 128] = jnp.where(
                        column == across + half * 128, 1.0, 0.0
                    ).astype(BF16)
            return carry

        lax.fori_loop(0, PEERS // 16, some, 0)

    def set_table(values):
        for a in range(4):
            for h in range(2):
                row = (a * 2 + h) * 8
                head, tail = split(values[a, :, h * 256 : h * 256 + 256])
                table[row : row + 8, :] = head.astype(F32)
                table[64 + row : 72 + row, :] = tail.astype(F32)

    def gather(first, count, write):
        down = lax.broadcasted_iota(jnp.int32, (64, LANES), 0)
        start = pl.multiple_of(first * LANES, LANES)
        rows = table[...].astype(BF16)
        found = jnp.dot(
            rows, hot_lanes[:, pl.ds(start, count * LANES)], preferred_element_type=F32
        )
        for i in range(count):
            block = found[0:64, i * LANES : (i + 1) * LANES] + found[64:128, i * LANES : (i + 1) * LANES]
            mask = down == jnp.broadcast_to(lo_ref[pl.ds(first + i, 1), :], (64, LANES))
            write(i, jnp.sum(jnp.where(mask, block, 0.0), axis=0, keepdims=True))

    def scatter(first, count, values, total):
        down = lax.broadcasted_iota(jnp.int32, (64, LANES), 0)
        zero = jnp.zeros((64, LANES), BF16)
        heads, tails = [], []
        for i in range(count):
            head, tail = split(values(i))
            mask = down == jnp.broadcast_to(lo_ref[pl.ds(first + i, 1), :], (64, LANES))
            heads.append(jnp.where(mask, jnp.broadcast_to(head, (64, LANES)), zero))
            tails.append(jnp.where(mask, jnp.broadcast_to(tail, (64, LANES)), zero))
        spread = jnp.concatenate(
            [jnp.concatenate(heads, axis=1), jnp.concatenate(tails, axis=1)], axis=0
        )
        start = pl.multiple_of(first * LANES, LANES)
        return total + jnp.dot(
            spread, hot_rows[pl.ds(start, count * LANES), :], preferred_element_type=F32
        )

    def send(phase, chunk, source, target):
        base = row_of(chunk)
        back_chunk = jnp.where(jnp.logical_and(chunk > 0, chunk < 3), 3 - chunk, chunk)
        for i in range(PER):
            slot = chunk * PER + i

            def away(i=i, slot=slot):
                pltpu.make_async_remote_copy(
                    src_ref=source.at[slot],
                    dst_ref=target.at[back_chunk * PER + MIRROR[i]],
                    send_sem=ssem.at[phase],
                    recv_sem=rsem.at[phase, back_chunk],
                    device_id=peer(base, i),
                    device_id_type=MESH,
                ).start()

            if i < PER - 1:
                away()
            else:
                pl.when(chunk < CHUNKS - 1)(away)

                @pl.when(chunk == CHUNKS - 1)
                def here(slot=slot):
                    pltpu.make_async_copy(
                        source.at[slot], target.at[slot], rsem.at[phase, chunk]
                    ).start()

    def wait_chunk(phase, chunk, target):
        block = target.at[pl.ds(chunk * PER, PER)]
        pltpu.make_async_copy(block, block, rsem.at[phase, chunk]).wait()

    def wait_sent(phase, source):
        block = source.at[pl.ds(0, PEERS - 1)]
        pltpu.make_async_copy(block, block, ssem.at[phase]).wait()

    def face_copies(phase):
        west = (lax.rem(gx + 15, 16), gy)
        east = (lax.rem(gx + 1, 16), gy)
        south = (gx, lax.rem(gy + 7, 8))
        north = (gx, lax.rem(gy + 1, 8))
        plan = (
            (face_x_out, face_x_in, 0, 1, west),
            (face_x_out, face_x_in, 1, 0, east),
            (face_y_out, face_y_in, 0, 1, south),
            (face_y_out, face_y_in, 1, 0, north),
        )
        copies = []
        for number, (out, into, side, other, device) in enumerate(plan):
            copies.append(
                pltpu.make_async_remote_copy(
                    src_ref=out.at[phase, side],
                    dst_ref=into.at[phase, other],
                    send_sem=face_ssem.at[phase, number],
                    recv_sem=face_rsem.at[phase, number],
                    device_id=device,
                    device_id_type=MESH,
                )
            )
        return copies

    def send_faces(phase, values):
        face_x_out[phase, 0] = values[0]
        face_x_out[phase, 1] = values[3]
        for a in range(4):
            face_y_out[phase, 0, a : a + 1, :] = values[a, 0:1, :]
            face_y_out[phase, 1, a : a + 1, :] = values[a, 7:8, :]
        for copy in face_copies(phase):
            copy.start()

    def beside(values, phase, a):
        plane = values[a]
        east = values[a + 1] if a < 3 else face_x_in[phase, 1]
        west = values[a - 1] if a > 0 else face_x_in[phase, 0]
        north = jnp.concatenate([plane[1:8], face_y_in[phase, 1, a : a + 1, :]], axis=0)
        south = jnp.concatenate([face_y_in[phase, 0, a : a + 1, :], plane[0:7]], axis=0)
        above = pltpu.roll(plane, 511, 1)
        below = pltpu.roll(plane, 1, 1)
        return plane, (east, west, north, south, above, below)

    set_table(keff)

    @each
    def own_ends(chunk):
        def put_k(i, row):
            send_a[chunk * PER + i, 0:1, :] = row

        index_lanes(0, chunk)
        gather(chunk * 2 * PER, PER, put_k)

    index_rows(0)

    pl.semaphore_wait(barrier, PEERS - 1)

    @each
    def send_ends(chunk):
        send(0, chunk, send_a, recv_a)

    send_faces(0, keff)

    @each
    def asked_ends(chunk):
        wait_chunk(0, chunk, recv_a)
        for i in range(PER):
            slot = chunk * PER + i
            cell_row[pl.ds(slot, 1), :] = recv_a[slot, 2:3, :].astype(jnp.int32)
        index_lanes(1, chunk)

        def put_k(i, row):
            send_b[chunk * PER + i, 0:1, :] = row

        gather(chunk * 2 * PER + PER, PER, put_k)
        send(1, chunk, send_b, recv_b)

    index_rows(1)
    for copy in face_copies(0):
        copy.wait_recv()

    inside_x = (gx > 0, gx < 15)
    inside_y = (gy > 0, gy < 7)
    for side in range(2):
        face_x_in[0, side] = jnp.where(inside_x[side], face_x_in[0, side], 0.0)
        face_y_in[0, side] = jnp.where(inside_y[side], face_y_in[0, side], 0.0)
    layer = lax.broadcasted_iota(jnp.int32, (8, 512), 1)
    for a in range(4):
        plane, others = beside(keff, 0, a)
        amount = diag_acc[a]
        for side in range(6):
            other = others[side]
            if side == 4:
                other = jnp.where(layer == 511, 0.0, other)
            if side == 5:
                other = jnp.where(layer == 0, 0.0, other)
            one = harmonic(plane, other, 0.8 if side >= 4 else 1.0)
            trans[side, a] = one
            amount = amount + one
        diagonal[a] = amount

    def asked_trans(chunk, total):
        first = chunk * 2 * PER + PER

        def value(i):
            slot = chunk * PER + i
            one = harmonic(recv_a[slot, 0:1, :], send_b[slot, 0:1, :], 1.0) * recv_a[slot, 1:2, :]
            fault_trans[pl.ds(first + i, 1), :] = one
            return one

        return scatter(first, PER, value, total)

    def own_trans(chunk, total):
        wait_chunk(1, chunk, recv_b)
        first = chunk * 2 * PER

        def value(i):
            slot = chunk * PER + i
            one = harmonic(send_a[slot, 0:1, :], recv_b[slot, 0:1, :], 1.0) * send_a[slot, 1:2, :]
            fault_trans[pl.ds(first + i, 1), :] = one
            return one

        return scatter(first, PER, value, total)

    nothing = jnp.zeros((128, 256), F32)
    total = lax.fori_loop(0, CHUNKS, asked_trans, nothing)
    total = lax.fori_loop(0, CHUNKS, own_trans, total)

    def place(total, a):
        halves = [
            total[(a * 2 + h) * 8 : (a * 2 + h) * 8 + 8, :]
            + total[64 + (a * 2 + h) * 8 : 64 + (a * 2 + h) * 8 + 8, :]
            for h in range(2)
        ]
        return jnp.concatenate(halves, axis=1)

    low = jnp.broadcast_to(low_ref[...], (8, 512))
    high = jnp.broadcast_to(high_ref[...], (8, 512))
    theta = (high + low) / 2.0
    delta = (high - low) / 2.0
    sigma = theta / delta
    for a in range(4):
        diagonal[a] = diagonal[a] + place(total, a)
        resid_ref[a] = right_ref[a]
        step_ref[a] = right_ref[a] / diagonal[a] / theta
        corr_ref[a] = jnp.zeros((8, 512), F32)

    def iteration(count, rho):
        phase = count + 2
        face_phase = count + 1
        send_faces(face_phase, step_ref)
        set_table(step_ref)
        source, target = send_p.at[count], recv_p.at[count]

        @each
        def ask(chunk):
            for kind in range(2):

                def put_p(i, row, kind=kind):
                    source[chunk * PER + i, kind : kind + 1, :] = row

                gather(chunk * 2 * PER + kind * PER, PER, put_p)
            send(phase, chunk, source, target)

        for copy in face_copies(face_phase):
            copy.wait_recv()
        for a in range(4):
            plane, others = beside(step_ref, face_phase, a)
            result = diag_acc[a] * plane
            for side in range(6):
                result = result + trans[side, a] * (plane - others[side])
            corr_ref[a] = corr_ref[a] + plane
            grid_part[a] = result

        def answer(chunk, total):
            wait_chunk(phase, chunk, target)
            first = chunk * 2 * PER

            def flux(i):
                slot, kind = chunk * PER + i % PER, i // PER
                return fault_trans[pl.ds(first + i, 1), :] * (
                    source[slot, kind : kind + 1, :] - target[slot, 1 - kind : 2 - kind, :]
                )

            return scatter(first, 2 * PER, flux, total)

        total = lax.fori_loop(0, CHUNKS, answer, nothing)
        rho_new = 1.0 / (2.0 * sigma - rho)
        for a in range(4):
            resid = resid_ref[a] - (grid_part[a] + place(total, a))
            resid_ref[a] = resid
            step_ref[a] = rho_new * rho * step_ref[a] + 2.0 * rho_new / delta * (resid / diagonal[a])
        return rho_new

    lax.fori_loop(0, ITERS, iteration, 1.0 / sigma)
    sent = [send_a, send_b] + [send_p.at[count] for count in range(ITERS)]
    for phase, source in enumerate(sent):
        wait_sent(phase, source)
    for phase in range(ITERS + 1):
        for copy in face_copies(phase):
            copy.wait_send()


def on_device(
    right_side,
    permeability,
    accumulation,
    active,
    fault_local,
    fault_remote,
    fault_count,
    fault_mult,
    low_bound,
    high_bound,
):
    shape = right_side.shape
    vmem = pl.BlockSpec(memory_space=pltpu.VMEM)
    smem = pl.BlockSpec(memory_space=pltpu.SMEM)
    rows = 2 * PEERS
    cells = pltpu.VMEM(shape, F32)
    return tuple(
        pl.pallas_call(
            kernel,
            out_shape=[jax.ShapeDtypeStruct(shape, F32)] * 2,
            in_specs=[vmem] * 7 + [smem] + [vmem] * 2,
            out_specs=[vmem] * 2,
            scratch_shapes=[
                cells,
                cells,
                cells,
                cells,
                pltpu.VMEM((6,) + shape, F32),
                pltpu.VMEM((PEERS, LANES), jnp.int32),
                pltpu.VMEM((rows, LANES), jnp.int32),
                pltpu.VMEM((256, rows * LANES), BF16),
                pltpu.VMEM((rows * LANES, 256), BF16),
                pltpu.VMEM((128, 256), F32),
                pltpu.VMEM((rows, LANES), F32),
                pltpu.VMEM((LANES, LANES), jnp.int32),
                cells,
                pltpu.VMEM((PEERS, 3, LANES), F32),
                pltpu.VMEM((PEERS, 3, LANES), F32),
                pltpu.VMEM((PEERS, 1, LANES), F32),
                pltpu.VMEM((PEERS, 1, LANES), F32),
                pltpu.VMEM((ITERS, PEERS, 2, LANES), F32),
                pltpu.VMEM((ITERS, PEERS, 2, LANES), F32),
                pltpu.VMEM((ITERS + 1, 2, 8, 512), F32),
                pltpu.VMEM((ITERS + 1, 2, 8, 512), F32),
                pltpu.VMEM((ITERS + 1, 2, 4, 512), F32),
                pltpu.VMEM((ITERS + 1, 2, 4, 512), F32),
                pltpu.SemaphoreType.DMA((ITERS + 2,)),
                pltpu.SemaphoreType.DMA((ITERS + 2, CHUNKS)),
                pltpu.SemaphoreType.DMA((ITERS + 1, 4)),
                pltpu.SemaphoreType.DMA((ITERS + 1, 4)),
            ],
            compiler_params=pltpu.CompilerParams(
                collective_id=0, has_side_effects=True, vmem_limit_bytes=56 * 2**20
            ),
        )(
            right_side,
            permeability,
            accumulation,
            active,
            fault_local.reshape(PEERS, LANES),
            fault_remote.reshape(PEERS, LANES),
            fault_mult.reshape(PEERS, LANES),
            fault_count,
            low_bound.reshape(1, 1),
            high_bound.reshape(1, 1),
        )
    )


def solution(mesh):
    in_specs = (
        P("gx", "gy", None),
        P("gx", "gy", None),
        P("gx", "gy", None),
        P("gx", "gy", None),
        P(("gx", "gy"), None, None),
        P(("gx", "gy"), None, None),
        P(("gx", "gy"), None),
        P(("gx", "gy"), None, None),
        P(),
        P(),
    )
    out_specs = (P("gx", "gy", None), P("gx", "gy", None))
    return jax.shard_map(
        on_device, mesh=mesh, in_specs=in_specs, out_specs=out_specs, check_vma=False
    )
```

```python
import functools

import jax
import jax.numpy as jnp
from jax import lax
from jax.experimental import pallas as pl
from jax.experimental.pallas import tpu as pltpu
from jax.sharding import PartitionSpec as P

ITERS = 3
PEERS = 128
CHUNKS = 4
PER = PEERS // CHUNKS
LANES = 128
MESH = pl.DeviceIdType.MESH
F32 = jnp.float32
BF16 = jnp.bfloat16


def harmonic(k_one, k_two, factor):
    total = k_one + k_two
    safe = jnp.where(total > 0.0, total, 1.0)
    return factor * (2.0 * (k_one * k_two)) / safe


def split(values):
    head = values.astype(BF16)
    tail = (values - head.astype(F32)).astype(BF16)
    return head, tail


def slot_plan():
    def hops(offset):
        return sum(min(d, 4 - d) for d in offset[:3])

    def opposite(offset):
        return tuple(-d % 4 for d in offset[:3]) + (offset[3],)

    offsets = [(x, z, y, c) for x in range(4) for z in range(4) for y in range(4) for c in range(2)]

    def rank(offset):
        pair = min(offset[:3], opposite(offset)[:3])
        alone = offset[:3] == opposite(offset)[:3]
        first = alone if hops(offset) == 2 else not alone
        return (-hops(offset), first, pair, offset[:3], 1 - offset[3])

    offsets.sort(key=rank)
    mirror = [offsets.index(opposite(offset)) for offset in offsets]
    assert all(slot // PER == back // PER for slot, back in enumerate(mirror))
    return offsets, mirror


OFFSETS, MIRROR = slot_plan()


def kernel(
    right_in,
    perm_in,
    acc_in,
    active_in,
    local_in,
    remote_in,
    mult_in,
    count_in,
    low_in,
    high_in,
    corr_ref,
    resid_ref,
    right_ref,
    perm_ref,
    acc_ref,
    active_ref,
    local_ref,
    remote_ref,
    mult_ref,
    count_ref,
    low_ref,
    high_ref,
    in_sem,
    keff,
    diag_acc,
    diagonal,
    step_ref,
    trans,
    cell_row,
    lo_ref,
    hot_lanes,
    hot_rows,
    table,
    fault_trans,
    turned,
    grid_part,
    send_a,
    recv_a,
    send_b,
    recv_b,
    send_p,
    recv_p,
    face_x_out,
    face_x_in,
    face_y_out,
    face_y_in,
    ssem,
    rsem,
    face_ssem,
    face_rsem,
):
    gx = lax.axis_index("gx")
    gy = lax.axis_index("gy")
    at_z = [lax.rem(lax.rem(gx, 4) + d, 4) for d in range(4)]
    at_y = [lax.rem(gy // 2 + d, 4) * 2 for d in range(4)]
    at_c = [lax.rem(lax.rem(gy, 2) + d, 2) for d in range(2)]

    at_x = [lax.rem(gx // 4 + d, 4) * 4 for d in range(4)]

    def peer(slot):
        dx, dz, dy, dc = OFFSETS[slot]
        return (at_x[dx] + at_z[dz], at_y[dy] + at_c[dc])

    pairs = (
        (local_in, local_ref),
        (remote_in, remote_ref),
        (mult_in, mult_ref),
        (count_in, count_ref),
        (perm_in, perm_ref),
        (active_in, active_ref),
        (acc_in, acc_ref),
        (right_in, right_ref),
        (low_in, low_ref),
        (high_in, high_ref),
    )

    def load(number):
        return pltpu.make_async_copy(*pairs[number], in_sem.at[number])

    def each(body):
        def one(chunk, carry):
            body(chunk)
            return carry

        lax.fori_loop(0, CHUNKS, one, 0)

    for number in range(10):
        load(number).start()
    barrier = pltpu.get_barrier_semaphore()

    for slot in range(PEERS - 1):
        pl.semaphore_signal(barrier, inc=1, device_id=peer(slot), device_id_type=MESH)

    for number in (0, 1, 2, 3):
        load(number).wait()

    lane = lax.broadcasted_iota(jnp.int32, (1, LANES), 1)
    for slot in range(PEERS):
        ox, oy = peer(slot)
        owner = ox * 8 + oy
        cell_row[slot : slot + 1, :] = local_ref[pl.ds(owner, 1), :]
        send_a[slot, 2:3, :] = remote_ref[pl.ds(owner, 1), :].astype(F32)
        mult = mult_ref[pl.ds(owner, 1), :]
        send_a[slot, 1:2, :] = jnp.where(lane < count_ref[0, owner], mult, 0.0)

    for number in range(4, 10):
        load(number).wait()
    keff[...] = jnp.where(active_ref[...] != 0, perm_ref[...], 0.0)
    diag_acc[...] = jnp.where(active_ref[...] != 0, acc_ref[...], 1.0)

    down = lax.broadcasted_iota(jnp.int32, (256, LANES), 0)
    across = lax.broadcasted_iota(jnp.int32, (LANES, LANES), 1)

    def index_lanes(kind, chunk):
        cells = cell_row[pl.ds(pl.multiple_of(chunk * PER, PER), PER), :]
        base = pl.multiple_of(chunk * 2 * PER + kind * PER, PER)
        lo_ref[pl.ds(base, PER), :] = (
            ((cells >> 12) * 2 + ((cells >> 8) & 1)) * 8 + ((cells >> 9) & 7)
        )

        def some(step, carry):
            for i in range(8):
                row = chunk * PER + step * 8 + i
                start = pl.multiple_of((base + step * 8 + i) * LANES, LANES)
                high = jnp.broadcast_to(cell_row[pl.ds(row, 1), :] & 255, (256, LANES))
                hot_lanes[:, pl.ds(start, LANES)] = jnp.where(high == down, 1.0, 0.0).astype(BF16)
            return carry

        lax.fori_loop(0, PER // 8, some, 0)

    def index_rows(kind):
        turned[...] = jnp.transpose(cell_row[...] & 255)

        def some(step, carry):
            shifted = pltpu.roll(turned[...], lax.rem(LANES - step * 16, LANES), 1)
            for i in range(16):
                slot = step * 16 + i
                column = jnp.broadcast_to(shifted[:, i : i + 1], (LANES, LANES))
                place = (slot // PER) * 2 * PER + kind * PER + lax.rem(slot, PER)
                start = pl.multiple_of(place * LANES, LANES)
                for half in range(2):
                    hot_rows[pl.ds(start, LANES), half * 128 : half * 128 + 128] = jnp.where(
                        column == across + half * 128, 1.0, 0.0
                    ).astype(BF16)
            return carry

        lax.fori_loop(0, PEERS // 16, some, 0)

    def set_table(values):
        for a in range(4):
            halves = jnp.concatenate([values[a, :, 0:256], values[a, :, 256:512]], axis=0)
            head, tail = split(halves)
            table[a * 16 : a * 16 + 16, :] = head
            table[64 + a * 16 : 80 + a * 16, :] = tail

    def gather(first, count, write):
        down = lax.broadcasted_iota(jnp.int32, (64, LANES), 0)
        start = pl.multiple_of(first * LANES, LANES)
        found = jnp.dot(
            table[...], hot_lanes[:, pl.ds(start, count * LANES)], preferred_element_type=F32
        )
        for i in range(count):
            block = found[0:64, i * LANES : (i + 1) * LANES] + found[64:128, i * LANES : (i + 1) * LANES]
            mask = down == jnp.broadcast_to(lo_ref[pl.ds(first + i, 1), :], (64, LANES))
            write(i, jnp.sum(jnp.where(mask, block, 0.0), axis=0, keepdims=True))

    def scatter(first, count, values, total):
        down = lax.broadcasted_iota(jnp.int32, (64, LANES), 0)
        zero = jnp.zeros((64, LANES), BF16)
        heads, tails = [], []
        for i in range(count):
            head, tail = split(values(i))
            mask = down == jnp.broadcast_to(lo_ref[pl.ds(first + i, 1), :], (64, LANES))
            heads.append(jnp.where(mask, jnp.broadcast_to(head, (64, LANES)), zero))
            tails.append(jnp.where(mask, jnp.broadcast_to(tail, (64, LANES)), zero))
        spread = jnp.concatenate(
            [jnp.concatenate(heads, axis=1), jnp.concatenate(tails, axis=1)], axis=0
        )
        start = pl.multiple_of(first * LANES, LANES)
        return total + jnp.dot(
            spread, hot_rows[pl.ds(start, count * LANES), :], preferred_element_type=F32
        )

    def send(phase, chunk, source, target):
        def part(number):
            for slot in range(number * PER, (number + 1) * PER):
                back = MIRROR[slot]
                if slot < PEERS - 1:
                    pltpu.make_async_remote_copy(
                        src_ref=source.at[slot],
                        dst_ref=target.at[back],
                        send_sem=ssem.at[phase],
                        recv_sem=rsem.at[phase, number],
                        device_id=peer(slot),
                        device_id_type=MESH,
                    ).start()
                else:
                    pltpu.make_async_copy(
                        source.at[slot], target.at[slot], rsem.at[phase, number]
                    ).start()

        for number in range(CHUNKS):
            pl.when(chunk == number)(functools.partial(part, number))

    def wait_chunk(phase, chunk, target):
        block = target.at[pl.ds(chunk * PER, PER)]
        pltpu.make_async_copy(block, block, rsem.at[phase, chunk]).wait()

    def wait_sent(phase, source):
        block = source.at[pl.ds(0, PEERS - 1)]
        pltpu.make_async_copy(block, block, ssem.at[phase]).wait()

    def face_copies(phase):
        west = (lax.rem(gx + 15, 16), gy)
        east = (lax.rem(gx + 1, 16), gy)
        south = (gx, lax.rem(gy + 7, 8))
        north = (gx, lax.rem(gy + 1, 8))
        plan = (
            (face_x_out, face_x_in, 0, 1, west),
            (face_x_out, face_x_in, 1, 0, east),
            (face_y_out, face_y_in, 0, 1, south),
            (face_y_out, face_y_in, 1, 0, north),
        )
        copies = []
        for number, (out, into, side, other, device) in enumerate(plan):
            copies.append(
                pltpu.make_async_remote_copy(
                    src_ref=out.at[phase, side],
                    dst_ref=into.at[phase, other],
                    send_sem=face_ssem.at[phase, number],
                    recv_sem=face_rsem.at[phase, number],
                    device_id=device,
                    device_id_type=MESH,
                )
            )
        return copies

    def send_faces(phase, values):
        face_x_out[phase, 0] = values[0]
        face_x_out[phase, 1] = values[3]
        for a in range(4):
            face_y_out[phase, 0, a : a + 1, :] = values[a, 0:1, :]
            face_y_out[phase, 1, a : a + 1, :] = values[a, 7:8, :]
        for copy in face_copies(phase):
            copy.start()

    def beside(values, phase, a):
        plane = values[a]
        east = values[a + 1] if a < 3 else face_x_in[phase, 1]
        west = values[a - 1] if a > 0 else face_x_in[phase, 0]
        north = jnp.concatenate([plane[1:8], face_y_in[phase, 1, a : a + 1, :]], axis=0)
        south = jnp.concatenate([face_y_in[phase, 0, a : a + 1, :], plane[0:7]], axis=0)
        above = pltpu.roll(plane, 511, 1)
        below = pltpu.roll(plane, 1, 1)
        return plane, (east, west, north, south, above, below)

    set_table(keff)

    @each
    def own_ends(chunk):
        def put_k(i, row):
            send_a[chunk * PER + i, 0:1, :] = row

        index_lanes(0, chunk)
        gather(chunk * 2 * PER, PER, put_k)

    index_rows(0)

    pl.semaphore_wait(barrier, PEERS - 1)

    @each
    def send_ends(chunk):
        send(0, chunk, send_a, recv_a)

    send_faces(0, keff)

    @each
    def asked_ends(chunk):
        wait_chunk(0, chunk, recv_a)
        for i in range(PER):
            slot = chunk * PER + i
            cell_row[pl.ds(slot, 1), :] = recv_a[slot, 2:3, :].astype(jnp.int32)
        index_lanes(1, chunk)

        def put_k(i, row):
            send_b[chunk * PER + i, 0:1, :] = row

        gather(chunk * 2 * PER + PER, PER, put_k)
        send(1, chunk, send_b, recv_b)

    index_rows(1)
    for copy in face_copies(0):
        copy.wait_recv()

    inside_x = (gx > 0, gx < 15)
    inside_y = (gy > 0, gy < 7)
    for side in range(2):
        face_x_in[0, side] = jnp.where(inside_x[side], face_x_in[0, side], 0.0)
        face_y_in[0, side] = jnp.where(inside_y[side], face_y_in[0, side], 0.0)
    layer = lax.broadcasted_iota(jnp.int32, (8, 512), 1)
    for a in range(4):
        plane, others = beside(keff, 0, a)
        amount = diag_acc[a]
        for side in range(6):
            other = others[side]
            if side == 4:
                other = jnp.where(layer == 511, 0.0, other)
            if side == 5:
                other = jnp.where(layer == 0, 0.0, other)
            one = harmonic(plane, other, 0.8 if side >= 4 else 1.0)
            trans[side, a] = one
            amount = amount + one
        diagonal[a] = amount

    def asked_trans(chunk, total):
        first = chunk * 2 * PER + PER

        def value(i):
            slot = chunk * PER + i
            one = harmonic(recv_a[slot, 0:1, :], send_b[slot, 0:1, :], 1.0) * recv_a[slot, 1:2, :]
            fault_trans[pl.ds(first + i, 1), :] = one
            return one

        return scatter(first, PER, value, total)

    def own_trans(chunk, total):
        wait_chunk(1, chunk, recv_b)
        first = chunk * 2 * PER

        def value(i):
            slot = chunk * PER + i
            one = harmonic(send_a[slot, 0:1, :], recv_b[slot, 0:1, :], 1.0) * send_a[slot, 1:2, :]
            fault_trans[pl.ds(first + i, 1), :] = one
            return one

        return scatter(first, PER, value, total)

    nothing = jnp.zeros((128, 256), F32)
    total = lax.fori_loop(0, CHUNKS, asked_trans, nothing)
    total = lax.fori_loop(0, CHUNKS, own_trans, total)

    def place(total, a):
        halves = [
            total[(a * 2 + h) * 8 : (a * 2 + h) * 8 + 8, :]
            + total[64 + (a * 2 + h) * 8 : 64 + (a * 2 + h) * 8 + 8, :]
            for h in range(2)
        ]
        return jnp.concatenate(halves, axis=1)

    low = jnp.full((8, 512), low_ref[0], F32)
    high = jnp.full((8, 512), high_ref[0], F32)
    theta = (high + low) / 2.0
    delta = (high - low) / 2.0
    sigma = theta / delta
    for a in range(4):
        diagonal[a] = diagonal[a] + place(total, a)
        resid_ref[a] = right_ref[a]
        step_ref[a] = right_ref[a] / diagonal[a] / theta
        corr_ref[a] = jnp.zeros((8, 512), F32)

    def iteration(count, rho):
        phase = count + 2
        face_phase = count + 1
        send_faces(face_phase, step_ref)
        set_table(step_ref)
        source, target = send_p.at[count], recv_p.at[count]

        @each
        def ask(chunk):
            def put_p(i, row):
                kind = i // PER
                source[chunk * PER + i % PER, kind : kind + 1, :] = row

            gather(chunk * 2 * PER, 2 * PER, put_p)
            send(phase, chunk, source, target)

        for copy in face_copies(face_phase):
            copy.wait_recv()
        for a in range(4):
            plane, others = beside(step_ref, face_phase, a)
            result = diag_acc[a] * plane
            for side in range(6):
                result = result + trans[side, a] * (plane - others[side])
            corr_ref[a] = corr_ref[a] + plane
            grid_part[a] = result

        def answer(chunk, total):
            wait_chunk(phase, chunk, target)
            first = chunk * 2 * PER

            def flux(i):
                slot, kind = chunk * PER + i % PER, i // PER
                return fault_trans[pl.ds(first + i, 1), :] * (
                    source[slot, kind : kind + 1, :] - target[slot, 1 - kind : 2 - kind, :]
                )

            return scatter(first, 2 * PER, flux, total)

        total = lax.fori_loop(0, CHUNKS, answer, nothing)
        rho_new = 1.0 / (2.0 * sigma - rho)
        for a in range(4):
            resid = resid_ref[a] - (grid_part[a] + place(total, a))
            resid_ref[a] = resid
            step_ref[a] = rho_new * rho * step_ref[a] + 2.0 * rho_new / delta * (resid / diagonal[a])
        return rho_new

    lax.fori_loop(0, ITERS, iteration, 1.0 / sigma)
    sent = [send_a, send_b] + [send_p.at[count] for count in range(ITERS)]
    for phase, source in enumerate(sent):
        wait_sent(phase, source)
    for phase in range(ITERS + 1):
        for copy in face_copies(phase):
            copy.wait_send()


def on_device(
    right_side,
    permeability,
    accumulation,
    active,
    fault_local,
    fault_remote,
    fault_count,
    fault_mult,
    low_bound,
    high_bound,
):
    shape = right_side.shape
    vmem = pl.BlockSpec(memory_space=pltpu.VMEM)
    rows = 2 * PEERS
    cells = pltpu.VMEM(shape, F32)
    return tuple(
        pl.pallas_call(
            kernel,
            out_shape=[jax.ShapeDtypeStruct(shape, F32)] * 2,
            in_specs=[pl.BlockSpec(memory_space=pl.ANY)] * 10,
            out_specs=[vmem] * 2,
            scratch_shapes=[
                cells,
                cells,
                cells,
                pltpu.VMEM(shape, jnp.int32),
                pltpu.VMEM((PEERS, LANES), jnp.int32),
                pltpu.VMEM((PEERS, LANES), jnp.int32),
                pltpu.VMEM((PEERS, LANES), F32),
                pltpu.SMEM((1, PEERS), jnp.int32),
                pltpu.SMEM((1,), F32),
                pltpu.SMEM((1,), F32),
                pltpu.SemaphoreType.DMA((10,)),
                cells,
                cells,
                cells,
                cells,
                pltpu.VMEM((6,) + shape, F32),
                pltpu.VMEM((PEERS, LANES), jnp.int32),
                pltpu.VMEM((rows, LANES), jnp.int32),
                pltpu.VMEM((256, rows * LANES), BF16),
                pltpu.VMEM((rows * LANES, 256), BF16),
                pltpu.VMEM((128, 256), BF16),
                pltpu.VMEM((rows, LANES), F32),
                pltpu.VMEM((LANES, LANES), jnp.int32),
                cells,
                pltpu.VMEM((PEERS, 3, LANES), F32),
                pltpu.VMEM((PEERS, 3, LANES), F32),
                pltpu.VMEM((PEERS, 1, LANES), F32),
                pltpu.VMEM((PEERS, 1, LANES), F32),
                pltpu.VMEM((ITERS, PEERS, 2, LANES), F32),
                pltpu.VMEM((ITERS, PEERS, 2, LANES), F32),
                pltpu.VMEM((ITERS + 1, 2, 8, 512), F32),
                pltpu.VMEM((ITERS + 1, 2, 8, 512), F32),
                pltpu.VMEM((ITERS + 1, 2, 4, 512), F32),
                pltpu.VMEM((ITERS + 1, 2, 4, 512), F32),
                pltpu.SemaphoreType.DMA((ITERS + 2,)),
                pltpu.SemaphoreType.DMA((ITERS + 2, CHUNKS)),
                pltpu.SemaphoreType.DMA((ITERS + 1, 4)),
                pltpu.SemaphoreType.DMA((ITERS + 1, 4)),
            ],
            compiler_params=pltpu.CompilerParams(
                collective_id=0, has_side_effects=True, vmem_limit_bytes=56 * 2**20
            ),
        )(
            right_side,
            permeability,
            accumulation,
            active,
            fault_local.reshape(PEERS, LANES),
            fault_remote.reshape(PEERS, LANES),
            fault_mult.reshape(PEERS, LANES),
            fault_count,
            low_bound,
            high_bound,
        )
    )


def solution(mesh):
    in_specs = (
        P("gx", "gy", None),
        P("gx", "gy", None),
        P("gx", "gy", None),
        P("gx", "gy", None),
        P(("gx", "gy"), None, None),
        P(("gx", "gy"), None, None),
        P(("gx", "gy"), None),
        P(("gx", "gy"), None, None),
        P(),
        P(),
    )
    out_specs = (P("gx", "gy", None), P("gx", "gy", None))
    return jax.shard_map(
        on_device, mesh=mesh, in_specs=in_specs, out_specs=out_specs, check_vma=False
    )
```

```python
import functools

import jax
import jax.numpy as jnp
from jax import lax
from jax.experimental import pallas as pl
from jax.experimental.pallas import tpu as pltpu
from jax.sharding import PartitionSpec as P

ITERS = 3
PEERS = 128
CHUNKS = 2
PER = PEERS // CHUNKS
LANES = 128
MESH = pl.DeviceIdType.MESH
F32 = jnp.float32
BF16 = jnp.bfloat16


def harmonic(k_one, k_two, factor):
    total = k_one + k_two
    safe = jnp.where(total > 0.0, total, 1.0)
    return factor * (2.0 * (k_one * k_two)) / safe


def split(values):
    head = values.astype(BF16)
    tail = (values - head.astype(F32)).astype(BF16)
    return head, tail


def slot_plan():
    def hops(offset):
        return sum(min(d, 4 - d) for d in offset[:3])

    def opposite(offset):
        return tuple(-d % 4 for d in offset[:3]) + (offset[3],)

    offsets = [(x, z, y, c) for x in range(4) for z in range(4) for y in range(4) for c in range(2)]

    def rank(offset):
        pair = min(offset[:3], opposite(offset)[:3])
        alone = offset[:3] == opposite(offset)[:3]
        first = alone if hops(offset) == 2 else not alone
        return (-hops(offset), first, pair, offset[:3], 1 - offset[3])

    offsets.sort(key=rank)
    mirror = [offsets.index(opposite(offset)) for offset in offsets]
    assert all(slot // PER == back // PER for slot, back in enumerate(mirror))
    return offsets, mirror


OFFSETS, MIRROR = slot_plan()


def kernel(
    right_in,
    perm_in,
    acc_in,
    active_in,
    local_in,
    remote_in,
    mult_in,
    count_in,
    low_in,
    high_in,
    corr_ref,
    resid_ref,
    right_ref,
    perm_ref,
    acc_ref,
    active_ref,
    local_ref,
    remote_ref,
    mult_ref,
    count_ref,
    low_ref,
    high_ref,
    in_sem,
    keff,
    diag_acc,
    diagonal,
    step_ref,
    trans,
    cell_row,
    lo_ref,
    hot_lanes,
    hot_rows,
    table,
    fault_trans,
    turned,
    grid_part,
    send_a,
    recv_a,
    send_b,
    recv_b,
    send_p,
    recv_p,
    face_x_out,
    face_x_in,
    face_y_out,
    face_y_in,
    ssem,
    rsem,
    face_ssem,
    face_rsem,
):
    gx = lax.axis_index("gx")
    gy = lax.axis_index("gy")
    at_z = [lax.rem(lax.rem(gx, 4) + d, 4) for d in range(4)]
    at_y = [lax.rem(gy // 2 + d, 4) * 2 for d in range(4)]
    at_c = [lax.rem(lax.rem(gy, 2) + d, 2) for d in range(2)]

    at_x = [lax.rem(gx // 4 + d, 4) * 4 for d in range(4)]

    at_xz = [[x + z for z in at_z] for x in at_x]
    at_yc = [[y + c for c in at_c] for y in at_y]

    def peer(slot):
        dx, dz, dy, dc = OFFSETS[slot]
        return (at_xz[dx][dz], at_yc[dy][dc])

    pairs = (
        (local_in, local_ref),
        (remote_in, remote_ref),
        (mult_in, mult_ref),
        (count_in, count_ref),
        (perm_in, perm_ref),
        (active_in, active_ref),
        (acc_in, acc_ref),
        (right_in, right_ref),
        (low_in, low_ref),
        (high_in, high_ref),
    )

    def load(number):
        return pltpu.make_async_copy(*pairs[number], in_sem.at[number])

    def each(body):
        def one(chunk, carry):
            body(chunk)
            return carry

        lax.fori_loop(0, CHUNKS, one, 0)

    for number in range(10):
        load(number).start()
    barrier = pltpu.get_barrier_semaphore()

    for slot in range(PEERS - 1):
        pl.semaphore_signal(barrier, inc=1, device_id=peer(slot), device_id_type=MESH)

    for number in (0, 1, 2, 3):
        load(number).wait()

    lane = lax.broadcasted_iota(jnp.int32, (1, LANES), 1)
    for slot in range(PEERS):
        ox, oy = peer(slot)
        owner = ox * 8 + oy
        cell_row[slot : slot + 1, :] = local_ref[pl.ds(owner, 1), :]
        send_a[slot, 2:3, :] = remote_ref[pl.ds(owner, 1), :].astype(F32)
        mult = mult_ref[pl.ds(owner, 1), :]
        send_a[slot, 1:2, :] = jnp.where(lane < count_ref[0, owner], mult, 0.0)

    for number in range(4, 10):
        load(number).wait()
    keff[...] = jnp.where(active_ref[...] != 0, perm_ref[...], 0.0)
    diag_acc[...] = jnp.where(active_ref[...] != 0, acc_ref[...], 1.0)

    down = lax.broadcasted_iota(jnp.int32, (256, LANES), 0)
    across = lax.broadcasted_iota(jnp.int32, (LANES, LANES), 1)

    def index_lanes(kind, chunk):
        cells = cell_row[pl.ds(pl.multiple_of(chunk * PER, PER), PER), :]
        base = pl.multiple_of(chunk * 2 * PER + kind * PER, PER)
        lo_ref[pl.ds(base, PER), :] = (
            ((cells >> 12) * 2 + ((cells >> 8) & 1)) * 8 + ((cells >> 9) & 7)
        )

        def some(step, carry):
            for i in range(8):
                row = chunk * PER + step * 8 + i
                start = pl.multiple_of((base + step * 8 + i) * LANES, LANES)
                high = jnp.broadcast_to(cell_row[pl.ds(row, 1), :] & 255, (256, LANES))
                hot_lanes[:, pl.ds(start, LANES)] = jnp.where(high == down, 1.0, 0.0).astype(BF16)
            return carry

        lax.fori_loop(0, PER // 8, some, 0)

    def index_rows(kind):
        turned[...] = jnp.transpose(cell_row[...] & 255)

        def some(step, carry):
            shifted = pltpu.roll(turned[...], lax.rem(LANES - step * 16, LANES), 1)
            for i in range(16):
                slot = step * 16 + i
                column = jnp.broadcast_to(shifted[:, i : i + 1], (LANES, LANES))
                place = (slot // PER) * 2 * PER + kind * PER + lax.rem(slot, PER)
                start = pl.multiple_of(place * LANES, LANES)
                for half in range(2):
                    hot_rows[pl.ds(start, LANES), half * 128 : half * 128 + 128] = jnp.where(
                        column == across + half * 128, 1.0, 0.0
                    ).astype(BF16)
            return carry

        lax.fori_loop(0, PEERS // 16, some, 0)

    def set_table(values):
        for a in range(4):
            halves = jnp.concatenate([values[a, :, 0:256], values[a, :, 256:512]], axis=0)
            head, tail = split(halves)
            table[a * 16 : a * 16 + 16, :] = head
            table[64 + a * 16 : 80 + a * 16, :] = tail

    def gather(first, count, write):
        down = lax.broadcasted_iota(jnp.int32, (64, LANES), 0)
        start = pl.multiple_of(first * LANES, LANES)
        found = jnp.dot(
            table[...], hot_lanes[:, pl.ds(start, count * LANES)], preferred_element_type=F32
        )
        for i in range(count):
            block = found[0:64, i * LANES : (i + 1) * LANES] + found[64:128, i * LANES : (i + 1) * LANES]
            mask = down == jnp.broadcast_to(lo_ref[pl.ds(first + i, 1), :], (64, LANES))
            write(i, jnp.sum(jnp.where(mask, block, 0.0), axis=0, keepdims=True))

    def scatter(first, count, values, total):
        down = lax.broadcasted_iota(jnp.int32, (64, LANES), 0)
        zero = jnp.zeros((64, LANES), BF16)
        heads, tails = [], []
        for i in range(count):
            head, tail = split(values(i))
            mask = down == jnp.broadcast_to(lo_ref[pl.ds(first + i, 1), :], (64, LANES))
            heads.append(jnp.where(mask, jnp.broadcast_to(head, (64, LANES)), zero))
            tails.append(jnp.where(mask, jnp.broadcast_to(tail, (64, LANES)), zero))
        spread = jnp.concatenate(
            [jnp.concatenate(heads, axis=1), jnp.concatenate(tails, axis=1)], axis=0
        )
        start = pl.multiple_of(first * LANES, LANES)
        return total + jnp.dot(
            spread, hot_rows[pl.ds(start, count * LANES), :], preferred_element_type=F32
        )

    def send(phase, chunk, source, target):
        def part(number):
            for slot in range(number * PER, (number + 1) * PER):
                back = MIRROR[slot]
                if slot < PEERS - 1:
                    pltpu.make_async_remote_copy(
                        src_ref=source.at[slot],
                        dst_ref=target.at[back],
                        send_sem=ssem.at[phase],
                        recv_sem=rsem.at[phase, number],
                        device_id=peer(slot),
                        device_id_type=MESH,
                    ).start()
                else:
                    pltpu.make_async_copy(
                        source.at[slot], target.at[slot], rsem.at[phase, number]
                    ).start()

        for number in range(CHUNKS):
            pl.when(chunk == number)(functools.partial(part, number))

    def wait_chunk(phase, chunk, target):
        block = target.at[pl.ds(chunk * PER, PER)]
        pltpu.make_async_copy(block, block, rsem.at[phase, chunk]).wait()

    def wait_sent(phase, source):
        block = source.at[pl.ds(0, PEERS - 1)]
        pltpu.make_async_copy(block, block, ssem.at[phase]).wait()

    def face_copies(phase):
        west = (lax.rem(gx + 15, 16), gy)
        east = (lax.rem(gx + 1, 16), gy)
        south = (gx, lax.rem(gy + 7, 8))
        north = (gx, lax.rem(gy + 1, 8))
        plan = (
            (face_x_out, face_x_in, 0, 1, west),
            (face_x_out, face_x_in, 1, 0, east),
            (face_y_out, face_y_in, 0, 1, south),
            (face_y_out, face_y_in, 1, 0, north),
        )
        copies = []
        for number, (out, into, side, other, device) in enumerate(plan):
            copies.append(
                pltpu.make_async_remote_copy(
                    src_ref=out.at[phase, side],
                    dst_ref=into.at[phase, other],
                    send_sem=face_ssem.at[phase, number],
                    recv_sem=face_rsem.at[phase, number],
                    device_id=device,
                    device_id_type=MESH,
                )
            )
        return copies

    def send_faces(phase, values):
        face_x_out[phase, 0] = values[0]
        face_x_out[phase, 1] = values[3]
        for a in range(4):
            face_y_out[phase, 0, a : a + 1, :] = values[a, 0:1, :]
            face_y_out[phase, 1, a : a + 1, :] = values[a, 7:8, :]
        for copy in face_copies(phase):
            copy.start()

    def beside(values, phase, a):
        plane = values[a]
        east = values[a + 1] if a < 3 else face_x_in[phase, 1]
        west = values[a - 1] if a > 0 else face_x_in[phase, 0]
        north = jnp.concatenate([plane[1:8], face_y_in[phase, 1, a : a + 1, :]], axis=0)
        south = jnp.concatenate([face_y_in[phase, 0, a : a + 1, :], plane[0:7]], axis=0)
        above = pltpu.roll(plane, 511, 1)
        below = pltpu.roll(plane, 1, 1)
        return plane, (east, west, north, south, above, below)

    set_table(keff)

    @each
    def own_ends(chunk):
        def put_k(i, row):
            send_a[chunk * PER + i, 0:1, :] = row

        index_lanes(0, chunk)
        gather(chunk * 2 * PER, PER, put_k)


    pl.semaphore_wait(barrier, PEERS - 1)

    send_faces(0, keff)

    @each
    def send_ends(chunk):
        send(0, chunk, send_a, recv_a)

    index_rows(0)
    for copy in face_copies(0):
        copy.wait_recv()

    inside_x = (gx > 0, gx < 15)
    inside_y = (gy > 0, gy < 7)
    for side in range(2):
        face_x_in[0, side] = jnp.where(inside_x[side], face_x_in[0, side], 0.0)
        face_y_in[0, side] = jnp.where(inside_y[side], face_y_in[0, side], 0.0)
    layer = lax.broadcasted_iota(jnp.int32, (8, 512), 1)
    for a in range(4):
        plane, others = beside(keff, 0, a)
        amount = diag_acc[a]
        for side in range(6):
            other = others[side]
            if side == 4:
                other = jnp.where(layer == 511, 0.0, other)
            if side == 5:
                other = jnp.where(layer == 0, 0.0, other)
            one = harmonic(plane, other, 0.8 if side >= 4 else 1.0)
            trans[side, a] = one
            amount = amount + one
        diagonal[a] = amount

    @each
    def asked_ends(chunk):
        wait_chunk(0, chunk, recv_a)
        for i in range(PER):
            slot = chunk * PER + i
            cell_row[pl.ds(slot, 1), :] = recv_a[slot, 2:3, :].astype(jnp.int32)
        index_lanes(1, chunk)

        def put_k(i, row):
            send_b[chunk * PER + i, 0:1, :] = row

        gather(chunk * 2 * PER + PER, PER, put_k)
        send(1, chunk, send_b, recv_b)

    index_rows(1)
    def asked_trans(chunk, total):
        first = chunk * 2 * PER + PER

        def value(i):
            slot = chunk * PER + i
            one = harmonic(recv_a[slot, 0:1, :], send_b[slot, 0:1, :], 1.0) * recv_a[slot, 1:2, :]
            fault_trans[pl.ds(first + i, 1), :] = one
            return one

        return scatter(first, PER, value, total)

    def own_trans(chunk, total):
        wait_chunk(1, chunk, recv_b)
        first = chunk * 2 * PER

        def value(i):
            slot = chunk * PER + i
            one = harmonic(send_a[slot, 0:1, :], recv_b[slot, 0:1, :], 1.0) * send_a[slot, 1:2, :]
            fault_trans[pl.ds(first + i, 1), :] = one
            return one

        return scatter(first, PER, value, total)

    nothing = jnp.zeros((128, 256), F32)
    total = lax.fori_loop(0, CHUNKS, asked_trans, nothing)
    total = lax.fori_loop(0, CHUNKS, own_trans, total)

    def place(total, a):
        halves = [
            total[(a * 2 + h) * 8 : (a * 2 + h) * 8 + 8, :]
            + total[64 + (a * 2 + h) * 8 : 64 + (a * 2 + h) * 8 + 8, :]
            for h in range(2)
        ]
        return jnp.concatenate(halves, axis=1)

    low = jnp.full((8, 512), low_ref[0], F32)
    high = jnp.full((8, 512), high_ref[0], F32)
    theta = (high + low) / 2.0
    delta = (high - low) / 2.0
    sigma = theta / delta
    for a in range(4):
        diagonal[a] = diagonal[a] + place(total, a)
        resid_ref[a] = right_ref[a]
        step_ref[a] = right_ref[a] / diagonal[a] / theta
        corr_ref[a] = jnp.zeros((8, 512), F32)

    def iteration(count, rho):
        phase = count + 2
        face_phase = count + 1
        send_faces(face_phase, step_ref)
        set_table(step_ref)
        source, target = send_p.at[count], recv_p.at[count]

        @each
        def ask(chunk):
            def put_p(i, row):
                kind = i // PER
                source[chunk * PER + i % PER, kind : kind + 1, :] = row

            gather(chunk * 2 * PER, 2 * PER, put_p)
            send(phase, chunk, source, target)

        for copy in face_copies(face_phase):
            copy.wait_recv()
        for a in range(4):
            plane, others = beside(step_ref, face_phase, a)
            result = diag_acc[a] * plane
            for side in range(6):
                result = result + trans[side, a] * (plane - others[side])
            corr_ref[a] = corr_ref[a] + plane
            grid_part[a] = result

        def answer(chunk, total):
            wait_chunk(phase, chunk, target)
            first = chunk * 2 * PER

            def flux(i):
                slot, kind = chunk * PER + i % PER, i // PER
                return fault_trans[pl.ds(first + i, 1), :] * (
                    source[slot, kind : kind + 1, :] - target[slot, 1 - kind : 2 - kind, :]
                )

            return scatter(first, 2 * PER, flux, total)

        total = lax.fori_loop(0, CHUNKS, answer, nothing)
        rho_new = 1.0 / (2.0 * sigma - rho)
        for a in range(4):
            resid = resid_ref[a] - (grid_part[a] + place(total, a))
            resid_ref[a] = resid
            step_ref[a] = rho_new * rho * step_ref[a] + 2.0 * rho_new / delta * (resid / diagonal[a])
        return rho_new

    lax.fori_loop(0, ITERS, iteration, 1.0 / sigma)
    sent = [send_a, send_b] + [send_p.at[count] for count in range(ITERS)]
    for phase, source in enumerate(sent):
        wait_sent(phase, source)
    for phase in range(ITERS + 1):
        for copy in face_copies(phase):
            copy.wait_send()


def on_device(
    right_side,
    permeability,
    accumulation,
    active,
    fault_local,
    fault_remote,
    fault_count,
    fault_mult,
    low_bound,
    high_bound,
):
    shape = right_side.shape
    vmem = pl.BlockSpec(memory_space=pltpu.VMEM)
    rows = 2 * PEERS
    cells = pltpu.VMEM(shape, F32)
    return tuple(
        pl.pallas_call(
            kernel,
            out_shape=[jax.ShapeDtypeStruct(shape, F32)] * 2,
            in_specs=[pl.BlockSpec(memory_space=pl.ANY)] * 10,
            out_specs=[vmem] * 2,
            scratch_shapes=[
                cells,
                cells,
                cells,
                pltpu.VMEM(shape, jnp.int32),
                pltpu.VMEM((PEERS, LANES), jnp.int32),
                pltpu.VMEM((PEERS, LANES), jnp.int32),
                pltpu.VMEM((PEERS, LANES), F32),
                pltpu.SMEM((1, PEERS), jnp.int32),
                pltpu.SMEM((1,), F32),
                pltpu.SMEM((1,), F32),
                pltpu.SemaphoreType.DMA((10,)),
                cells,
                cells,
                cells,
                cells,
                pltpu.VMEM((6,) + shape, F32),
                pltpu.VMEM((PEERS, LANES), jnp.int32),
                pltpu.VMEM((rows, LANES), jnp.int32),
                pltpu.VMEM((256, rows * LANES), BF16),
                pltpu.VMEM((rows * LANES, 256), BF16),
                pltpu.VMEM((128, 256), BF16),
                pltpu.VMEM((rows, LANES), F32),
                pltpu.VMEM((LANES, LANES), jnp.int32),
                cells,
                pltpu.VMEM((PEERS, 3, LANES), F32),
                pltpu.VMEM((PEERS, 3, LANES), F32),
                pltpu.VMEM((PEERS, 1, LANES), F32),
                pltpu.VMEM((PEERS, 1, LANES), F32),
                pltpu.VMEM((ITERS, PEERS, 2, LANES), F32),
                pltpu.VMEM((ITERS, PEERS, 2, LANES), F32),
                pltpu.VMEM((ITERS + 1, 2, 8, 512), F32),
                pltpu.VMEM((ITERS + 1, 2, 8, 512), F32),
                pltpu.VMEM((ITERS + 1, 2, 4, 512), F32),
                pltpu.VMEM((ITERS + 1, 2, 4, 512), F32),
                pltpu.SemaphoreType.DMA((ITERS + 2,)),
                pltpu.SemaphoreType.DMA((ITERS + 2, CHUNKS)),
                pltpu.SemaphoreType.DMA((ITERS + 1, 4)),
                pltpu.SemaphoreType.DMA((ITERS + 1, 4)),
            ],
            compiler_params=pltpu.CompilerParams(
                collective_id=0, has_side_effects=True, vmem_limit_bytes=56 * 2**20
            ),
        )(
            right_side,
            permeability,
            accumulation,
            active,
            fault_local.reshape(PEERS, LANES),
            fault_remote.reshape(PEERS, LANES),
            fault_mult.reshape(PEERS, LANES),
            fault_count,
            low_bound,
            high_bound,
        )
    )


def solution(mesh):
    in_specs = (
        P("gx", "gy", None),
        P("gx", "gy", None),
        P("gx", "gy", None),
        P("gx", "gy", None),
        P(("gx", "gy"), None, None),
        P(("gx", "gy"), None, None),
        P(("gx", "gy"), None),
        P(("gx", "gy"), None, None),
        P(),
        P(),
    )
    out_specs = (P("gx", "gy", None), P("gx", "gy", None))
    return jax.shard_map(
        on_device, mesh=mesh, in_specs=in_specs, out_specs=out_specs, check_vma=False
    )
```

```python
import functools

import jax
import jax.numpy as jnp
from jax import lax
from jax.experimental import pallas as pl
from jax.experimental.pallas import tpu as pltpu
from jax.sharding import PartitionSpec as P

ITERS = 3
PEERS = 128
CHUNKS = 2
PER = PEERS // CHUNKS
LANES = 128
MESH = pl.DeviceIdType.MESH
F32 = jnp.float32
BF16 = jnp.bfloat16


def harmonic(k_one, k_two, factor):
    total = k_one + k_two
    safe = jnp.where(total > 0.0, total, 1.0)
    return factor * (2.0 * (k_one * k_two)) / safe


def split(values):
    head = values.astype(BF16)
    tail = (values - head.astype(F32)).astype(BF16)
    return head, tail


def slot_plan():
    def hops(offset):
        return sum(min(d, 4 - d) for d in offset[:3])

    def opposite(offset):
        return tuple(-d % 4 for d in offset[:3]) + (offset[3],)

    offsets = [(x, z, y, c) for x in range(4) for z in range(4) for y in range(4) for c in range(2)]

    def rank(offset):
        pair = min(offset[:3], opposite(offset)[:3])
        alone = offset[:3] == opposite(offset)[:3]
        first = alone if hops(offset) == 2 else not alone
        return (-hops(offset), first, pair, offset[:3], 1 - offset[3])

    offsets.sort(key=rank)
    mirror = [offsets.index(opposite(offset)) for offset in offsets]
    assert all(slot // PER == back // PER for slot, back in enumerate(mirror))
    return offsets, mirror


OFFSETS, MIRROR = slot_plan()


def kernel(
    right_in,
    perm_in,
    acc_in,
    active_in,
    local_in,
    remote_in,
    mult_in,
    count_in,
    low_in,
    high_in,
    corr_ref,
    resid_ref,
    right_ref,
    perm_ref,
    acc_ref,
    active_ref,
    local_ref,
    remote_ref,
    mult_ref,
    count_ref,
    low_ref,
    high_ref,
    in_sem,
    keff,
    diag_acc,
    diagonal,
    step_ref,
    trans,
    cell_row,
    lo_ref,
    hot_lanes,
    hot_rows,
    table,
    fault_trans,
    turned,
    grid_part,
    send_a,
    recv_a,
    send_b,
    recv_b,
    send_p,
    recv_p,
    face_x_out,
    face_x_in,
    face_y_out,
    face_y_in,
    ssem,
    rsem,
    face_ssem,
    face_rsem,
):
    gx = lax.axis_index("gx")
    gy = lax.axis_index("gy")
    at_z = [lax.rem(lax.rem(gx, 4) + d, 4) for d in range(4)]
    at_y = [lax.rem(gy // 2 + d, 4) * 2 for d in range(4)]
    at_c = [lax.rem(lax.rem(gy, 2) + d, 2) for d in range(2)]

    at_x = [lax.rem(gx // 4 + d, 4) * 4 for d in range(4)]

    at_xz = [[x + z for z in at_z] for x in at_x]
    at_yc = [[y + c for c in at_c] for y in at_y]

    def peer(slot):
        dx, dz, dy, dc = OFFSETS[slot]
        return (at_xz[dx][dz], at_yc[dy][dc])

    pairs = (
        (local_in, local_ref),
        (remote_in, remote_ref),
        (mult_in, mult_ref),
        (count_in, count_ref),
        (perm_in, perm_ref),
        (active_in, active_ref),
        (acc_in, acc_ref),
        (right_in, right_ref),
        (low_in, low_ref),
        (high_in, high_ref),
    )

    def load(number):
        return pltpu.make_async_copy(*pairs[number], in_sem.at[number])

    def each(body):
        def one(chunk, carry):
            body(chunk)
            return carry

        lax.fori_loop(0, CHUNKS, one, 0)

    for number in range(10):
        load(number).start()
    barrier = pltpu.get_barrier_semaphore()

    for slot in range(PEERS - 1):
        pl.semaphore_signal(barrier, inc=1, device_id=peer(slot), device_id_type=MESH)

    for number in (0, 1, 2, 3):
        load(number).wait()

    lane = lax.broadcasted_iota(jnp.int32, (1, LANES), 1)
    for slot in range(PEERS):
        ox, oy = peer(slot)
        owner = ox * 8 + oy
        cell_row[slot : slot + 1, :] = local_ref[pl.ds(owner, 1), :]
        send_a[slot, 2:3, :] = remote_ref[pl.ds(owner, 1), :].astype(F32)
        mult = mult_ref[pl.ds(owner, 1), :]
        send_a[slot, 1:2, :] = jnp.where(lane < count_ref[0, owner], mult, 0.0)

    for number in range(4, 10):
        load(number).wait()
    keff[...] = jnp.where(active_ref[...] != 0, perm_ref[...], 0.0)
    diag_acc[...] = jnp.where(active_ref[...] != 0, acc_ref[...], 1.0)

    down = lax.broadcasted_iota(jnp.int32, (256, LANES), 0)
    across = lax.broadcasted_iota(jnp.int32, (LANES, LANES), 1)

    def index_lanes(kind, chunk):
        cells = cell_row[pl.ds(pl.multiple_of(chunk * PER, PER), PER), :]
        base = pl.multiple_of(chunk * 2 * PER + kind * PER, PER)
        lo_ref[pl.ds(base, PER), :] = (
            ((cells >> 12) * 2 + ((cells >> 8) & 1)) * 8 + ((cells >> 9) & 7)
        )

        def some(step, carry):
            for i in range(8):
                row = chunk * PER + step * 8 + i
                start = pl.multiple_of((base + step * 8 + i) * LANES, LANES)
                high = jnp.broadcast_to(cell_row[pl.ds(row, 1), :] & 255, (256, LANES))
                hot_lanes[:, pl.ds(start, LANES)] = jnp.where(high == down, 1.0, 0.0).astype(BF16)
            return carry

        lax.fori_loop(0, PER // 8, some, 0)

    def index_rows(kind):
        turned[...] = jnp.transpose(cell_row[...] & 255)

        def some(step, carry):
            shifted = pltpu.roll(turned[...], lax.rem(LANES - step * 16, LANES), 1)
            for i in range(16):
                slot = step * 16 + i
                column = jnp.broadcast_to(shifted[:, i : i + 1], (LANES, LANES))
                place = (slot // PER) * 2 * PER + kind * PER + lax.rem(slot, PER)
                start = pl.multiple_of(place * LANES, LANES)
                for half in range(2):
                    hot_rows[pl.ds(start, LANES), half * 128 : half * 128 + 128] = jnp.where(
                        column == across + half * 128, 1.0, 0.0
                    ).astype(BF16)
            return carry

        lax.fori_loop(0, PEERS // 16, some, 0)

    def set_table(values):
        for a in range(4):
            halves = jnp.concatenate([values[a, :, 0:256], values[a, :, 256:512]], axis=0)
            head, tail = split(halves)
            table[a * 16 : a * 16 + 16, :] = head
            table[64 + a * 16 : 80 + a * 16, :] = tail

    def gather(first, count, write):
        down = lax.broadcasted_iota(jnp.int32, (64, LANES), 0)
        start = pl.multiple_of(first * LANES, LANES)
        found = jnp.dot(
            table[...], hot_lanes[:, pl.ds(start, count * LANES)], preferred_element_type=F32
        )
        for i in range(count):
            block = found[0:64, i * LANES : (i + 1) * LANES] + found[64:128, i * LANES : (i + 1) * LANES]
            mask = down == jnp.broadcast_to(lo_ref[pl.ds(first + i, 1), :], (64, LANES))
            write(i, jnp.sum(jnp.where(mask, block, 0.0), axis=0, keepdims=True))

    def scatter(first, count, values, total):
        down = lax.broadcasted_iota(jnp.int32, (64, LANES), 0)
        zero = jnp.zeros((64, LANES), BF16)
        heads, tails = [], []
        for i in range(count):
            head, tail = split(values(i))
            mask = down == jnp.broadcast_to(lo_ref[pl.ds(first + i, 1), :], (64, LANES))
            heads.append(jnp.where(mask, jnp.broadcast_to(head, (64, LANES)), zero))
            tails.append(jnp.where(mask, jnp.broadcast_to(tail, (64, LANES)), zero))
        spread = jnp.concatenate(
            [jnp.concatenate(heads, axis=1), jnp.concatenate(tails, axis=1)], axis=0
        )
        start = pl.multiple_of(first * LANES, LANES)
        return total + jnp.dot(
            spread, hot_rows[pl.ds(start, count * LANES), :], preferred_element_type=F32
        )

    def send(phase, chunk, source, target):
        def part(number):
            for slot in range(number * PER, (number + 1) * PER):
                back = MIRROR[slot]
                if slot < PEERS - 1:
                    pltpu.make_async_remote_copy(
                        src_ref=source.at[slot],
                        dst_ref=target.at[back],
                        send_sem=ssem.at[phase],
                        recv_sem=rsem.at[phase, number],
                        device_id=peer(slot),
                        device_id_type=MESH,
                    ).start()
                else:
                    pltpu.make_async_copy(
                        source.at[slot], target.at[slot], rsem.at[phase, number]
                    ).start()

        for number in range(CHUNKS):
            pl.when(chunk == number)(functools.partial(part, number))

    def wait_chunk(phase, chunk, target):
        block = target.at[pl.ds(chunk * PER, PER)]
        pltpu.make_async_copy(block, block, rsem.at[phase, chunk]).wait()

    def wait_sent(phase, source):
        block = source.at[pl.ds(0, PEERS - 1)]
        pltpu.make_async_copy(block, block, ssem.at[phase]).wait()

    def face_copies(phase):
        west = (lax.rem(gx + 15, 16), gy)
        east = (lax.rem(gx + 1, 16), gy)
        south = (gx, lax.rem(gy + 7, 8))
        north = (gx, lax.rem(gy + 1, 8))
        plan = (
            (face_x_out, face_x_in, 0, 1, west),
            (face_x_out, face_x_in, 1, 0, east),
            (face_y_out, face_y_in, 0, 1, south),
            (face_y_out, face_y_in, 1, 0, north),
        )
        copies = []
        for number, (out, into, side, other, device) in enumerate(plan):
            copies.append(
                pltpu.make_async_remote_copy(
                    src_ref=out.at[phase, side],
                    dst_ref=into.at[phase, other],
                    send_sem=face_ssem.at[phase, number],
                    recv_sem=face_rsem.at[phase, number],
                    device_id=device,
                    device_id_type=MESH,
                )
            )
        return copies

    def send_faces(phase, values):
        face_x_out[phase, 0] = values[0]
        face_x_out[phase, 1] = values[3]
        for a in range(4):
            face_y_out[phase, 0, a : a + 1, :] = values[a, 0:1, :]
            face_y_out[phase, 1, a : a + 1, :] = values[a, 7:8, :]
        for copy in face_copies(phase):
            copy.start()

    def beside(values, phase, a):
        plane = values[a]
        east = values[a + 1] if a < 3 else face_x_in[phase, 1]
        west = values[a - 1] if a > 0 else face_x_in[phase, 0]
        north = jnp.concatenate([plane[1:8], face_y_in[phase, 1, a : a + 1, :]], axis=0)
        south = jnp.concatenate([face_y_in[phase, 0, a : a + 1, :], plane[0:7]], axis=0)
        above = pltpu.roll(plane, 511, 1)
        below = pltpu.roll(plane, 1, 1)
        return plane, (east, west, north, south, above, below)

    set_table(keff)

    @each
    def own_ends(chunk):
        def put_k(i, row):
            send_a[chunk * PER + i, 0:1, :] = row

        index_lanes(0, chunk)
        gather(chunk * 2 * PER, PER, put_k)


    pl.semaphore_wait(barrier, PEERS - 1)

    send_faces(0, keff)

    @each
    def send_ends(chunk):
        send(0, chunk, send_a, recv_a)

    index_rows(0)
    for copy in face_copies(0):
        copy.wait_recv()

    inside_x = (gx > 0, gx < 15)
    inside_y = (gy > 0, gy < 7)
    for side in range(2):
        face_x_in[0, side] = jnp.where(inside_x[side], face_x_in[0, side], 0.0)
        face_y_in[0, side] = jnp.where(inside_y[side], face_y_in[0, side], 0.0)
    layer = lax.broadcasted_iota(jnp.int32, (8, 512), 1)
    for a in range(4):
        plane, others = beside(keff, 0, a)
        amount = diag_acc[a]
        for side in range(6):
            other = others[side]
            if side == 4:
                other = jnp.where(layer == 511, 0.0, other)
            if side == 5:
                other = jnp.where(layer == 0, 0.0, other)
            one = harmonic(plane, other, 0.8 if side >= 4 else 1.0)
            trans[side, a] = one
            amount = amount + one
        diagonal[a] = amount

    @each
    def asked_ends(chunk):
        wait_chunk(0, chunk, recv_a)
        for i in range(PER):
            slot = chunk * PER + i
            cell_row[pl.ds(slot, 1), :] = recv_a[slot, 2:3, :].astype(jnp.int32)
        index_lanes(1, chunk)

        def put_k(i, row):
            send_b[chunk * PER + i, 0:1, :] = row

        gather(chunk * 2 * PER + PER, PER, put_k)
        send(1, chunk, send_b, recv_b)

    index_rows(1)
    def asked_trans(chunk, total):
        first = chunk * 2 * PER + PER
        slots = pl.ds(chunk * PER, PER)
        fault_trans[pl.ds(first, PER), :] = (
            harmonic(recv_a[slots, 0, :], send_b[slots, 0, :], 1.0) * recv_a[slots, 1, :]
        )

        def value(i):
            return fault_trans[pl.ds(first + i, 1), :]

        return scatter(first, PER, value, total)

    def own_trans(chunk, total):
        wait_chunk(1, chunk, recv_b)
        first = chunk * 2 * PER
        slots = pl.ds(chunk * PER, PER)
        fault_trans[pl.ds(first, PER), :] = (
            harmonic(send_a[slots, 0, :], recv_b[slots, 0, :], 1.0) * send_a[slots, 1, :]
        )

        def value(i):
            return fault_trans[pl.ds(first + i, 1), :]

        return scatter(first, PER, value, total)

    nothing = jnp.zeros((128, 256), F32)
    total = lax.fori_loop(0, CHUNKS, asked_trans, nothing)
    total = lax.fori_loop(0, CHUNKS, own_trans, total)

    def place(total, a):
        halves = [
            total[(a * 2 + h) * 8 : (a * 2 + h) * 8 + 8, :]
            + total[64 + (a * 2 + h) * 8 : 64 + (a * 2 + h) * 8 + 8, :]
            for h in range(2)
        ]
        return jnp.concatenate(halves, axis=1)

    low = jnp.full((8, 512), low_ref[0], F32)
    high = jnp.full((8, 512), high_ref[0], F32)
    theta = (high + low) / 2.0
    delta = (high - low) / 2.0
    sigma = theta / delta
    for a in range(4):
        diagonal[a] = diagonal[a] + place(total, a)
        resid_ref[a] = right_ref[a]
        step_ref[a] = right_ref[a] / diagonal[a] / theta
        corr_ref[a] = jnp.zeros((8, 512), F32)

    def iteration(count, rho):
        phase = count + 2
        face_phase = count + 1
        send_faces(face_phase, step_ref)
        set_table(step_ref)
        source, target = send_p.at[count], recv_p.at[count]

        @each
        def ask(chunk):
            def put_p(i, row):
                kind = i // PER
                source[chunk * PER + i % PER, kind : kind + 1, :] = row

            gather(chunk * 2 * PER, 2 * PER, put_p)
            send(phase, chunk, source, target)

        for copy in face_copies(face_phase):
            copy.wait_recv()
        for a in range(4):
            plane, others = beside(step_ref, face_phase, a)
            result = diag_acc[a] * plane
            for side in range(6):
                result = result + trans[side, a] * (plane - others[side])
            corr_ref[a] = corr_ref[a] + plane
            grid_part[a] = result

        def answer(chunk, total):
            wait_chunk(phase, chunk, target)
            first = chunk * 2 * PER

            def flux(i):
                slot, kind = chunk * PER + i % PER, i // PER
                return fault_trans[pl.ds(first + i, 1), :] * (
                    source[slot, kind : kind + 1, :] - target[slot, 1 - kind : 2 - kind, :]
                )

            return scatter(first, 2 * PER, flux, total)

        total = lax.fori_loop(0, CHUNKS, answer, nothing)
        rho_new = 1.0 / (2.0 * sigma - rho)
        for a in range(4):
            resid = resid_ref[a] - (grid_part[a] + place(total, a))
            resid_ref[a] = resid
            step_ref[a] = rho_new * rho * step_ref[a] + 2.0 * rho_new / delta * (resid / diagonal[a])
        return rho_new

    lax.fori_loop(0, ITERS, iteration, 1.0 / sigma)
    sent = [send_a, send_b] + [send_p.at[count] for count in range(ITERS)]
    for phase, source in enumerate(sent):
        wait_sent(phase, source)
    for phase in range(ITERS + 1):
        for copy in face_copies(phase):
            copy.wait_send()


def on_device(
    right_side,
    permeability,
    accumulation,
    active,
    fault_local,
    fault_remote,
    fault_count,
    fault_mult,
    low_bound,
    high_bound,
):
    shape = right_side.shape
    vmem = pl.BlockSpec(memory_space=pltpu.VMEM)
    rows = 2 * PEERS
    cells = pltpu.VMEM(shape, F32)
    return tuple(
        pl.pallas_call(
            kernel,
            out_shape=[jax.ShapeDtypeStruct(shape, F32)] * 2,
            in_specs=[pl.BlockSpec(memory_space=pl.ANY)] * 10,
            out_specs=[vmem] * 2,
            scratch_shapes=[
                cells,
                cells,
                cells,
                pltpu.VMEM(shape, jnp.int32),
                pltpu.VMEM((PEERS, LANES), jnp.int32),
                pltpu.VMEM((PEERS, LANES), jnp.int32),
                pltpu.VMEM((PEERS, LANES), F32),
                pltpu.SMEM((1, PEERS), jnp.int32),
                pltpu.SMEM((1,), F32),
                pltpu.SMEM((1,), F32),
                pltpu.SemaphoreType.DMA((10,)),
                cells,
                cells,
                cells,
                cells,
                pltpu.VMEM((6,) + shape, F32),
                pltpu.VMEM((PEERS, LANES), jnp.int32),
                pltpu.VMEM((rows, LANES), jnp.int32),
                pltpu.VMEM((256, rows * LANES), BF16),
                pltpu.VMEM((rows * LANES, 256), BF16),
                pltpu.VMEM((128, 256), BF16),
                pltpu.VMEM((rows, LANES), F32),
                pltpu.VMEM((LANES, LANES), jnp.int32),
                cells,
                pltpu.VMEM((PEERS, 3, LANES), F32),
                pltpu.VMEM((PEERS, 3, LANES), F32),
                pltpu.VMEM((PEERS, 1, LANES), F32),
                pltpu.VMEM((PEERS, 1, LANES), F32),
                pltpu.VMEM((ITERS, PEERS, 2, LANES), F32),
                pltpu.VMEM((ITERS, PEERS, 2, LANES), F32),
                pltpu.VMEM((ITERS + 1, 2, 8, 512), F32),
                pltpu.VMEM((ITERS + 1, 2, 8, 512), F32),
                pltpu.VMEM((ITERS + 1, 2, 4, 512), F32),
                pltpu.VMEM((ITERS + 1, 2, 4, 512), F32),
                pltpu.SemaphoreType.DMA((ITERS + 2,)),
                pltpu.SemaphoreType.DMA((ITERS + 2, CHUNKS)),
                pltpu.SemaphoreType.DMA((ITERS + 1, 4)),
                pltpu.SemaphoreType.DMA((ITERS + 1, 4)),
            ],
            compiler_params=pltpu.CompilerParams(
                collective_id=0, has_side_effects=True, vmem_limit_bytes=56 * 2**20
            ),
        )(
            right_side,
            permeability,
            accumulation,
            active,
            fault_local.reshape(PEERS, LANES),
            fault_remote.reshape(PEERS, LANES),
            fault_mult.reshape(PEERS, LANES),
            fault_count,
            low_bound,
            high_bound,
        )
    )


def solution(mesh):
    in_specs = (
        P("gx", "gy", None),
        P("gx", "gy", None),
        P("gx", "gy", None),
        P("gx", "gy", None),
        P(("gx", "gy"), None, None),
        P(("gx", "gy"), None, None),
        P(("gx", "gy"), None),
        P(("gx", "gy"), None, None),
        P(),
        P(),
    )
    out_specs = (P("gx", "gy", None), P("gx", "gy", None))
    return jax.shard_map(
        on_device, mesh=mesh, in_specs=in_specs, out_specs=out_specs, check_vma=False
    )
```
